512 devices in a mesh: fsdp: 32 (over z, y_lo, core), mp: 16 (over y_hi, x).
Axes of the slice: x: 4, y: 8 (y_hi: 4, y_lo: 2; y = y_hi * 2 + y_lo), z: 8, core: 2. Of those that a mesh axis runs over, the one named last changes fastest.
Arguments:
- normed_tokens: bfloat16 [8192, 6144], P('fsdp', 'mp'), may hold values from -6 to 6
- up_weight: bfloat16 [6144, 12288], P('fsdp', 'mp'), may hold values from -0.078125 to 0.078125
- adapter_down: bfloat16 [6144, 64], replicated, may hold values from -0.078125 to 0.078125
- adapter_up: bfloat16 [64, 12288], replicated, may hold values from -0.0546875 to 0.0546875
- act_grad: bfloat16 [8192, 12288], P('fsdp', 'mp'), may hold values from -3 to 3
Outputs:
- normed_grad: bfloat16 [8192, 6144], P('fsdp', 'mp')
- down_grad: bfloat16 [6144, 64], P('mp')
- up_grad: bfloat16 [64, 12288], P(None, 'mp')
The draws below stay inside these ranges and needn't reach their ends.
All inputs are finite; a program needn't handle non-finite values.
Results may differ from the reference program's by a relative error of at most 0.019.
Values may be sent and summed in bfloat16 or wider, within the bound.
No kernel may reach another device: no remote copies, remote signals or barrier semaphores. Data moves between devices by JAX's collectives and lax.ppermute only.
A program may use at most 64 MiB of HBM per device.

```python
import jax
import jax.numpy as jnp
from jax import lax

D = 6144
HIDDEN_SIZE = 12288
RANK = 64
TOKENS = 8192
HID_BLOCK = 768


def block_levels(stream_key, dims, pieces, smallest, top_value):
    level, own = 1.0, jax.random.fold_in(stream_key, 6)
    for axis_at, shards_of in pieces:
        steps = jnp.exp(jax.random.uniform(jax.random.fold_in(own, axis_at), (shards_of,), jnp.float32, smallest / len(pieces), top_value / len(pieces)))
        level = level * jnp.repeat(steps, dims[axis_at] // shards_of).reshape([-1 if axis == axis_at else 1 for axis in range(len(dims))])
    return level


def normal_values(key, dims, deviation, most, pieces=(), dtype=jnp.bfloat16):
    array = jax.random.normal(key, dims, jnp.float32) * deviation
    if len(pieces) > 0:
        array = block_levels(key, dims, pieces, -0.22, 0.18) * array
    return jnp.clip(array, min=-most, max=most).astype(dtype)


def setup_inputs(seed: int = 0) -> dict:
    streams_of = jax.random.split(jax.random.key(seed), 6)
    normed_tokens = normal_values(streams_of[0], (TOKENS, D), 1.0, 6.0, ((0, 32), (1, 16)))
    up_weight = normal_values(streams_of[1], (D, HIDDEN_SIZE), D ** -0.5, 0.078125, ((0, 32), (1, 16)))
    adapter_down = normal_values(streams_of[2], (D, RANK), D ** -0.5, 0.078125)
    adapter_up = normal_values(streams_of[3], (RANK, HIDDEN_SIZE), HIDDEN_SIZE ** -0.5, 0.0546875)
    act_grad = normal_values(streams_of[4], (TOKENS, HIDDEN_SIZE), 0.5, 3.0, ((0, 32), (1, 16)))
    return dict(normed_tokens=normed_tokens, up_weight=up_weight, adapter_down=adapter_down, adapter_up=adapter_up, act_grad=act_grad)


adapter_scale = 2.0


def gelu_slope(preact):
    normal_cdf = 0.5 * (1.0 + jax.scipy.special.erf(preact * 0.7071067811865476))
    density = jnp.exp(-0.5 * preact * preact) * 0.3989422804014327
    return normal_cdf + preact * density


def reference(normed_tokens, up_weight, adapter_down, adapter_up, act_grad):
    lowrank = jnp.dot(normed_tokens, adapter_down, preferred_element_type=jnp.float32).astype(jnp.bfloat16)
    preact = jnp.dot(normed_tokens, up_weight, preferred_element_type=jnp.float32) + adapter_scale * jnp.dot(lowrank, adapter_up, preferred_element_type=jnp.float32)
    slope_grad = (act_grad.astype(jnp.float32) * gelu_slope(preact)).astype(jnp.bfloat16)
    up_grad = (adapter_scale * jnp.dot(lowrank.T, slope_grad, preferred_element_type=jnp.float32)).astype(jnp.bfloat16)
    rank_grad = (adapter_scale * jnp.dot(slope_grad, adapter_up.T, preferred_element_type=jnp.float32)).astype(jnp.bfloat16)
    down_grad = jnp.dot(normed_tokens.T, rank_grad, preferred_element_type=jnp.float32).astype(jnp.bfloat16)
    frozen_grad = jnp.zeros((TOKENS, D), jnp.float32)
    for column_block in range(HIDDEN_SIZE // HID_BLOCK):
        first = column_block * HID_BLOCK
        product = jnp.dot(slope_grad[:, first:first + HID_BLOCK], up_weight[:, first:first + HID_BLOCK].T, preferred_element_type=jnp.float32)
        rounded = lax.optimization_barrier(product.astype(jnp.bfloat16)).astype(jnp.float32)
        frozen_grad = frozen_grad + rounded
    normed_grad = (frozen_grad + jnp.dot(rank_grad, adapter_down.T, preferred_element_type=jnp.float32)).astype(jnp.bfloat16)
    return (normed_grad, down_grad, up_grad)
```

```python
import jax
import jax.numpy as jnp
from jax import lax
from jax.sharding import PartitionSpec as P

adapter_scale = 2.0

Z, YL, C = 8, 2, 2
YH, X = 4, 4


def gelu_slope(preact):
    normal_cdf = 0.5 * (1.0 + jax.scipy.special.erf(preact * 0.7071067811865476))
    density = jnp.exp(-0.5 * preact * preact) * 0.3989422804014327
    return normal_cdf + preact * density


def contract(left, right, left_dim, right_dim):
    return lax.dot_general(
        left, right, (((left_dim,), (right_dim,)), ((), ())), preferred_element_type=jnp.float32
    )


def mp_send(value, step):
    pairs = []
    for m in range(YH * X):
        y, x = step(m // X, m % X)
        pairs.append((m, (y % YH) * X + x % X))
    return lax.ppermute(value, "mp", pairs)


def fsdp_send(value, step):
    pairs = []
    for f in range(Z * YL * C):
        z, y, c = step(f // (YL * C), f // C % YL, f % C)
        pairs.append((f, (z % Z) * YL * C + y * C + c))
    return lax.ppermute(value, "fsdp", pairs)


def y_up(value):
    return mp_send(value, lambda y, x: (y + 1, x))


def y_down(value):
    return mp_send(value, lambda y, x: (y - 1, x))


def x_up(value):
    return mp_send(value, lambda y, x: (y, x + 1))


def x_down(value):
    return mp_send(value, lambda y, x: (y, x - 1))


def ring_gather(value, up, down):
    half = value.shape[0] // 2
    previous, following = up(value), down(value)
    opposite = jnp.concatenate([up(previous[:half]), down(following[half:])], axis=0)
    return [value, following, opposite, previous]


def ring_scatter(parts, up, down):
    half = parts[2].shape[0] // 2
    from_previous = up(parts[2][:half])
    from_next = down(parts[2][half:])
    f32 = jnp.float32
    to_next = jnp.concatenate(
        [(parts[1][:half].astype(f32) + from_previous.astype(f32)).astype(jnp.bfloat16), parts[1][half:]], axis=0
    )
    to_previous = jnp.concatenate(
        [parts[3][:half], (parts[3][half:].astype(f32) + from_next.astype(f32)).astype(jnp.bfloat16)], axis=0
    )
    return parts[0].astype(f32) + up(to_next).astype(f32) + down(to_previous).astype(f32)


def sum_mp(value):
    for step in (
        lambda y, x: (y, x ^ 1),
        lambda y, x: (y, 3 - x),
        lambda y, x: (y ^ 1, x),
        lambda y, x: (3 - y, x),
    ):
        value = value + mp_send(value, step)
    return value


def sum_fsdp(value):
    for step in (
        lambda z, y, c: (z, y, c ^ 1),
        lambda z, y, c: (z, y ^ 1, c),
        lambda z, y, c: (z ^ 1, y, c),
        lambda z, y, c: (z ^ 2, y, c),
        lambda z, y, c: (7 - z, y, c),
    ):
        value = value + fsdp_send(value, step)
    return value


def body(normed_tokens, up_weight, adapter_down, adapter_up, act_grad):
    tok_rows, local_width = normed_tokens.shape
    hidden_cols = up_weight.shape[1]
    model_index = lax.axis_index("mp")
    y_hi, x_at = model_index >> 2, model_index & 3

    gathered = lax.all_gather(up_weight, "fsdp", axis=0, tiled=True)

    along_y = jnp.concatenate(ring_gather(normed_tokens, y_up, y_down), axis=1)
    along_x = ring_gather(along_y, x_up, x_down)
    whole_rows = jnp.zeros((tok_rows, local_width * YH * X), jnp.bfloat16)
    for q in range(X):
        for r in range(YH):
            at = (((y_hi + r) & 3) * X + ((x_at + q) & 3)) * local_width
            block = along_x[q][:, r * local_width : (r + 1) * local_width]
            whole_rows = lax.dynamic_update_slice_in_dim(whole_rows, block, at, 1)

    lowrank = jnp.dot(whole_rows, adapter_down, preferred_element_type=jnp.float32).astype(
        jnp.bfloat16
    )
    up_columns = lax.dynamic_slice_in_dim(adapter_up, model_index * hidden_cols, hidden_cols, 1)
    down_rows = lax.dynamic_slice_in_dim(adapter_down, model_index * local_width, local_width, 0)
    frozen_pre = jnp.dot(whole_rows, gathered, preferred_element_type=jnp.float32)
    preact = frozen_pre + adapter_scale * jnp.dot(
        lowrank, up_columns, preferred_element_type=jnp.float32
    )
    slope_grad = (act_grad.astype(jnp.float32) * gelu_slope(preact)).astype(jnp.bfloat16)

    rank_part = adapter_scale * contract(up_columns, slope_grad, 1, 1)
    rank_grad = sum_mp(rank_part).astype(jnp.bfloat16)
    up_local = adapter_scale * contract(lowrank, slope_grad, 0, 0)
    up_grad = sum_fsdp(up_local).astype(jnp.bfloat16)
    down_local = contract(rank_grad, normed_tokens, 1, 0)
    down_grad = sum_fsdp(down_local).astype(jnp.bfloat16).T

    frozen_term = contract(slope_grad, gathered, 1, 1).astype(jnp.bfloat16)
    by_x = []
    for q in range(X):
        blocks = []
        for r in range(YH):
            at = (((y_hi + r) & 3) * X + ((x_at + q) & 3)) * local_width
            blocks.append(lax.dynamic_slice_in_dim(frozen_term, at, local_width, 1))
        by_x.append(jnp.concatenate(blocks, axis=1))
    over_x = ring_scatter(by_x, x_up, x_down).astype(jnp.bfloat16)
    by_y = [over_x[:, r * local_width : (r + 1) * local_width] for r in range(YH)]
    summed = ring_scatter(by_y, y_up, y_down)
    normed_grad = (summed + contract(rank_grad, down_rows, 0, 1)).astype(jnp.bfloat16)
    return (normed_grad, down_grad, up_grad)


def solution(mesh):
    placed = (P("fsdp", "mp"), P("fsdp", "mp"), P(), P(), P("fsdp", "mp"))
    return jax.shard_map(
        body,
        mesh=mesh,
        in_specs=placed,
        out_specs=(P("fsdp", "mp"), P("mp", None), P(None, "mp")),
        check_vma=False,
    )
```

```python
import functools

import jax
import jax.numpy as jnp
from jax import lax
from jax.experimental import pallas as pl
from jax.experimental.pallas import tpu as pltpu
from jax.sharding import PartitionSpec as P

adapter_scale = 2.0
f32, bf16 = jnp.float32, jnp.bfloat16

Z, YL, C = 8, 2, 2
YH, X = 4, 4


def gelu_slope(preact):
    normal_cdf = 0.5 * (1.0 + lax.erf(preact * 0.7071067811865476))
    density = jnp.exp(-0.5 * preact * preact) * 0.3989422804014327
    return normal_cdf + preact * density


def contract(left, right, left_dim, right_dim):
    return lax.dot_general(
        left, right, (((left_dim,), (right_dim,)), ((), ())), preferred_element_type=f32
    )


def send(value, step):
    pairs = []
    for device in range(Z * YL * C * YH * X):
        f, m = device // (YH * X), device % (YH * X)
        z, yl, c, yh, x = step(f // (YL * C), f // C % YL, f % C, m // X, m % X)
        pairs.append((device, ((z * YL + yl) * C + c) * YH * X + yh * X + x))
    return lax.ppermute(value, ("fsdp", "mp"), pairs)


def first(c):
    return 1 if c else 3


def second(c):
    return 3 if c else 1


y_first = functools.partial(send, step=lambda z, yl, c, yh, x: (z, yl, c, yh ^ first(c), x))
y_second = functools.partial(send, step=lambda z, yl, c, yh, x: (z, yl, c, yh ^ second(c), x))
x_first = functools.partial(send, step=lambda z, yl, c, yh, x: (z, yl, c, yh, x ^ first(c)))
x_second = functools.partial(send, step=lambda z, yl, c, yh, x: (z, yl, c, yh, x ^ second(c)))


def block_copy(table, w, held, sems, p):
    width = w.shape[0] // 16
    source = w.at[pl.ds(pl.multiple_of(table[p] * width, width), width)]
    return pltpu.make_async_copy(source, held.at[pl.ds(p * width, width)], sems.at[p])


def main_kernel(table, xa, xb, w, down_t, up, act, slope_out, rank_out, up_out, away, held, acc, low, sems):
    width = w.shape[0] // 16
    wide = 2 * width
    for p in range(16):
        block_copy(table, w, held, sems, p).start()

    acc[...] = jnp.zeros_like(acc)
    low[...] = jnp.zeros_like(low)

    def gather_half(x_ref, base):
        def step(k, carry):
            at = pl.multiple_of(k * wide, wide)
            p = base + 2 * k
            block_copy(table, w, held, sems, p).wait()
            block_copy(table, w, held, sems, p + 1).wait()
            x = x_ref[:, pl.ds(at, wide)]
            rows = pl.ds(pl.multiple_of(p * width, wide), wide)
            acc[...] += jnp.dot(x, held[rows], preferred_element_type=f32)
            for half in range(2):
                there = pl.ds(pl.multiple_of(table[p + half] * width, width), width)
                low[...] += contract(down_t[:, there], x[:, half * width : (half + 1) * width], 1, 1)
            return carry

        lax.fori_loop(0, 4, step, 0)

    gather_half(xa, 0)
    gather_half(xb, 8)

    low_t = low[...]
    lowrank_t, lowrank = low_t.astype(bf16), low_t.T.astype(bf16)
    preact = acc[...] + adapter_scale * jnp.dot(lowrank, up[...], preferred_element_type=f32)
    slope = (act[...].astype(f32) * gelu_slope(preact)).astype(bf16)
    slope_out[...] = slope
    rank_out[...] = adapter_scale * contract(up[...], slope, 1, 1)
    up_out[...] = adapter_scale * jnp.dot(lowrank_t, slope, preferred_element_type=f32)

    def term(k, carry):
        at = pl.multiple_of(k * wide, wide)
        rows = pl.ds(pl.multiple_of(8 * width + k * wide, wide), wide)
        away[:, pl.ds(at, wide)] = contract(slope_out[...], held[rows], 1, 1).astype(bf16)
        return carry

    lax.fori_loop(0, 4, term, 0)


VMEM = pl.BlockSpec(memory_space=pltpu.VMEM)
SMEM = pl.BlockSpec(memory_space=pltpu.SMEM)
HBM = pl.BlockSpec(memory_space=pltpu.HBM)


def forward(table, xa, xb, w, down_t, up, act):
    rows, rank, hidden = xa.shape[0], down_t.shape[0], w.shape[1]
    return pl.pallas_call(
        main_kernel,
        out_shape=(
            jax.ShapeDtypeStruct((rows, hidden), bf16),
            jax.ShapeDtypeStruct((rank, rows), f32),
            jax.ShapeDtypeStruct((rank, hidden), f32),
            jax.ShapeDtypeStruct(xa.shape, bf16),
        ),
        in_specs=[SMEM, VMEM, VMEM, HBM, VMEM, VMEM, VMEM],
        out_specs=(VMEM, VMEM, VMEM, VMEM),
        scratch_shapes=[
            pltpu.VMEM(w.shape, bf16),
            pltpu.VMEM((rows, hidden), f32),
            pltpu.VMEM((rank, rows), f32),
            pltpu.SemaphoreType.DMA((16,)),
        ],
        compiler_params=pltpu.CompilerParams(vmem_limit_bytes=56 * 2**20),
        cost_estimate=pl.CostEstimate(
            flops=3 * rows * w.shape[0] * hidden, bytes_accessed=14 * 2**20, transcendentals=0
        ),
        name="forward",
    )(table, xa, xb, w, down_t, up, act)


def kept_kernel(table, slope, w, out, held, sems):
    width = w.shape[0] // 16
    wide = 2 * width
    for p in range(8):
        block_copy(table, w, held, sems, p).start()

    def term(k, carry):
        block_copy(table, w, held, sems, 2 * k).wait()
        block_copy(table, w, held, sems, 2 * k + 1).wait()
        at = pl.multiple_of(k * wide, wide)
        out[:, pl.ds(at, wide)] = contract(slope[...], held[pl.ds(at, wide)], 1, 1).astype(bf16)
        return carry

    lax.fori_loop(0, 4, term, 0)


def kept_half(table, slope, w):
    rows, hidden = slope.shape
    half = w.shape[0] // 2
    return pl.pallas_call(
        kept_kernel,
        out_shape=jax.ShapeDtypeStruct((rows, half), bf16),
        in_specs=[SMEM, VMEM, HBM],
        out_specs=VMEM,
        scratch_shapes=[pltpu.VMEM((half, hidden), bf16), pltpu.SemaphoreType.DMA((8,))],
        compiler_params=pltpu.CompilerParams(vmem_limit_bytes=56 * 2**20),
        cost_estimate=pl.CostEstimate(
            flops=2 * rows * half * hidden, bytes_accessed=7 * 2**20, transcendentals=0
        ),
        name="kept_half",
    )(table, slope, w)


def widen(value):
    return value.astype(f32)


def pair_sum(value, *meetings):
    for meet in meetings:
        value = value + meet(value)
    return value


def rounded_sum(value, meet):
    rounded = value.astype(bf16)
    return widen(rounded) + widen(send(rounded, meet))


def body(normed_tokens, up_weight, adapter_down, adapter_up, act_grad):
    width = normed_tokens.shape[1]
    hidden = up_weight.shape[1]
    model_index = lax.axis_index("mp")
    core = lax.axis_index("fsdp") & 1
    y_hi, x_at = model_index >> 2, model_index & 3
    one, two = 3 - 2 * core, 1 + 2 * core

    step = [0 * core, one, two, 0 * core + 2]
    table = jnp.stack([((y_hi ^ step[r]) << 2) | (x_at ^ step[q]) for q in range(4) for r in range(4)])

    gathered = lax.all_gather(up_weight, "fsdp", axis=0, tiled=True)

    pair = jnp.concatenate([normed_tokens, y_first(normed_tokens)], axis=1)
    column = jnp.concatenate([pair, y_second(pair)], axis=1)
    near = jnp.concatenate([column, x_first(column)], axis=1)
    far = x_second(near)

    up_columns = lax.dynamic_slice_in_dim(adapter_up, model_index * hidden, hidden, 1)
    slope_grad, rank_part, up_local, away = forward(
        table, near, far, gathered, adapter_down.T, up_columns, act_grad
    )

    over_x = x_second(away)
    kept = kept_half(table, slope_grad, gathered)
    rank_sum = pair_sum(rank_part, y_first, y_second)
    over_x, kept, rank_sum = lax.optimization_barrier((over_x, kept, rank_sum))

    half = 4 * width
    to_next = (widen(kept[:, half:]) + widen(over_x[:, half:])).astype(bf16)
    over_next = x_first(to_next)
    rank_sum = pair_sum(rank_sum, x_first, x_second)
    over_next, rank_sum = lax.optimization_barrier((over_next, rank_sum))

    rank_grad = rank_sum.astype(bf16)
    own = widen(kept[:, :half]) + widen(over_x[:, :half]) + widen(over_next)
    own, to_y = own[:, : 2 * width], own[:, 2 * width :].astype(bf16)
    over_y = y_second(to_y)
    down_local = jnp.dot(rank_grad, normed_tokens, preferred_element_type=f32)
    grads = jnp.concatenate([up_local, down_local], axis=1)
    grads = rounded_sum(grads, lambda z, yl, c, yh, x: (z ^ 1, yl, c, yh, x))
    grads = rounded_sum(grads, lambda z, yl, c, yh, x: (z ^ 3, yl, c, yh, x))
    over_y, grads = lax.optimization_barrier((over_y, grads))

    own = own + widen(over_y)
    own, to_y = own[:, :width], own[:, width:].astype(bf16)
    over_y = y_first(to_y)
    grads = rounded_sum(grads, lambda z, yl, c, yh, x: (z ^ 7, yl, c, yh, x))
    grads = rounded_sum(grads, lambda z, yl, c, yh, x: (z, yl ^ 1, c, yh, x))
    grads = rounded_sum(grads, lambda z, yl, c, yh, x: (z, yl, c ^ 1, yh, x))
    summed = own + widen(over_y)
    up_grad, down_grad = grads[:, :hidden].astype(bf16), grads[:, hidden:].astype(bf16).T

    down_rows = lax.dynamic_slice_in_dim(adapter_down, model_index * width, width, 0)
    normed_grad = (summed + contract(rank_grad, down_rows, 0, 1)).astype(bf16)
    return (normed_grad, down_grad, up_grad)


def solution(mesh):
    placed = (P("fsdp", "mp"), P("fsdp", "mp"), P(), P(), P("fsdp", "mp"))
    return jax.shard_map(
        body,
        mesh=mesh,
        in_specs=placed,
        out_specs=(P("fsdp", "mp"), P("mp", None), P(None, "mp")),
        check_vma=False,
    )
```

```python
import functools

import jax
import jax.numpy as jnp
from jax import lax
from jax.experimental import pallas as pl
from jax.experimental.pallas import tpu as pltpu
from jax.sharding import PartitionSpec as P

adapter_scale = 2.0
f32, bf16 = jnp.float32, jnp.bfloat16

Z, YL, C = 8, 2, 2
YH, X = 4, 4


def gelu_slope(preact):
    normal_cdf = 0.5 * (1.0 + lax.erf(preact * 0.7071067811865476))
    density = jnp.exp(-0.5 * preact * preact) * 0.3989422804014327
    return normal_cdf + preact * density


def contract(left, right, left_dim, right_dim):
    return lax.dot_general(
        left, right, (((left_dim,), (right_dim,)), ((), ())), preferred_element_type=f32
    )


def send(value, step):
    pairs = []
    for device in range(Z * YL * C * YH * X):
        f, m = device // (YH * X), device % (YH * X)
        z, yl, c, yh, x = step(f // (YL * C), f // C % YL, f % C, m // X, m % X)
        pairs.append((device, ((z * YL + yl) * C + c) * YH * X + yh * X + x))
    return lax.ppermute(value, ("fsdp", "mp"), pairs)


def first(c):
    return 1 if c else 3


def second(c):
    return 3 if c else 1


y_first = functools.partial(send, step=lambda z, yl, c, yh, x: (z, yl, c, yh ^ first(c), x))
y_second = functools.partial(send, step=lambda z, yl, c, yh, x: (z, yl, c, yh ^ second(c), x))
x_first = functools.partial(send, step=lambda z, yl, c, yh, x: (z, yl, c, yh, x ^ first(c)))
x_second = functools.partial(send, step=lambda z, yl, c, yh, x: (z, yl, c, yh, x ^ second(c)))


def block_copy(table, w, held, sems, p):
    width = w.shape[0] // 16
    source = w.at[pl.ds(pl.multiple_of(table[p] * width, width), width)]
    return pltpu.make_async_copy(source, held.at[pl.ds(p * width, width)], sems.at[p])


def lowrank_kernel(table, xa, xb, down_t, up, low_out, term_out):
    width = xa.shape[1] // 8
    low = jnp.zeros(low_out.shape, f32)
    for p in range(16):
        there = pl.ds(pl.multiple_of(table[p] * width, width), width)
        x_ref = xa if p < 8 else xb
        x = x_ref[:, p % 8 * width : (p % 8 + 1) * width]
        low += contract(down_t[:, there], x, 1, 1)
    low_out[...] = low.astype(bf16)
    lowrank = low.T.astype(bf16)
    term_out[...] = adapter_scale * jnp.dot(lowrank, up[...], preferred_element_type=f32)


def main_kernel(table, xa, xb, w, low_t, term, up, act, slope_out, rank_out, up_out, away, held, acc, sems):
    width = w.shape[0] // 16
    wide = 2 * width
    for p in range(16):
        block_copy(table, w, held, sems, p).start()

    acc[...] = term[...]
    for k in range(8):
        block_copy(table, w, held, sems, 2 * k).wait()
        block_copy(table, w, held, sems, 2 * k + 1).wait()
        x_ref = xa if k < 4 else xb
        x = x_ref[:, k % 4 * wide : (k % 4 + 1) * wide]
        acc[...] += jnp.dot(x, held[k * wide : (k + 1) * wide], preferred_element_type=f32)

    slope = (act[...].astype(f32) * gelu_slope(acc[...])).astype(bf16)
    slope_out[...] = slope
    rank_out[...] = (adapter_scale * contract(up[...], slope, 1, 1)).astype(bf16)
    up_out[...] = (adapter_scale * jnp.dot(low_t[...], slope, preferred_element_type=f32)).astype(bf16)

    for k in range(4):
        rows = held[(4 + k) * wide : (5 + k) * wide]
        away[:, k * wide : (k + 1) * wide] = contract(slope, rows, 1, 1).astype(bf16)


VMEM = pl.BlockSpec(memory_space=pltpu.VMEM)
SMEM = pl.BlockSpec(memory_space=pltpu.SMEM)
HBM = pl.BlockSpec(memory_space=pltpu.HBM)


def lowrank_terms(table, xa, xb, down_t, up):
    rows, rank, hidden = xa.shape[0], up.shape[0], up.shape[1]
    return pl.pallas_call(
        lowrank_kernel,
        out_shape=(
            jax.ShapeDtypeStruct((rank, rows), bf16),
            jax.ShapeDtypeStruct((rows, hidden), f32),
        ),
        in_specs=[SMEM, VMEM, VMEM, VMEM, VMEM],
        out_specs=(VMEM, VMEM),
        compiler_params=pltpu.CompilerParams(vmem_limit_bytes=56 * 2**20),
        cost_estimate=pl.CostEstimate(
            flops=2 * rows * rank * 16 * xa.shape[1], bytes_accessed=5 * 2**20, transcendentals=0
        ),
        name="lowrank_terms",
    )(table, xa, xb, down_t, up)


def forward(table, xa, xb, w, low_t, term, up, act):
    rows, rank, hidden = xa.shape[0], up.shape[0], w.shape[1]
    return pl.pallas_call(
        main_kernel,
        out_shape=(
            jax.ShapeDtypeStruct((rows, hidden), bf16),
            jax.ShapeDtypeStruct((rank, rows), bf16),
            jax.ShapeDtypeStruct((rank, hidden), bf16),
            jax.ShapeDtypeStruct(xa.shape, bf16),
        ),
        in_specs=[SMEM, VMEM, VMEM, HBM, VMEM, VMEM, VMEM, VMEM],
        out_specs=(VMEM, VMEM, VMEM, VMEM),
        scratch_shapes=[
            pltpu.VMEM(w.shape, bf16),
            pltpu.VMEM((rows, hidden), f32),
            pltpu.SemaphoreType.DMA((16,)),
        ],
        compiler_params=pltpu.CompilerParams(vmem_limit_bytes=56 * 2**20),
        cost_estimate=pl.CostEstimate(
            flops=3 * rows * w.shape[0] * hidden, bytes_accessed=14 * 2**20, transcendentals=0
        ),
        name="forward",
    )(table, xa, xb, w, low_t, term, up, act)


def kept_kernel(table, slope, w, out, held, sems):
    width = w.shape[0] // 16
    wide = 2 * width
    for p in range(8):
        block_copy(table, w, held, sems, p).start()

    def term(k, carry):
        block_copy(table, w, held, sems, 2 * k).wait()
        block_copy(table, w, held, sems, 2 * k + 1).wait()
        at = pl.multiple_of(k * wide, wide)
        out[:, pl.ds(at, wide)] = contract(slope[...], held[pl.ds(at, wide)], 1, 1).astype(bf16)
        return carry

    lax.fori_loop(0, 4, term, 0)


def kept_half(table, slope, w):
    rows, hidden = slope.shape
    half = w.shape[0] // 2
    return pl.pallas_call(
        kept_kernel,
        out_shape=jax.ShapeDtypeStruct((rows, half), bf16),
        in_specs=[SMEM, VMEM, HBM],
        out_specs=VMEM,
        scratch_shapes=[pltpu.VMEM((half, hidden), bf16), pltpu.SemaphoreType.DMA((8,))],
        compiler_params=pltpu.CompilerParams(vmem_limit_bytes=56 * 2**20),
        cost_estimate=pl.CostEstimate(
            flops=2 * rows * half * hidden, bytes_accessed=7 * 2**20, transcendentals=0
        ),
        name="kept_half",
    )(table, slope, w)


def widen(value):
    return value.astype(f32)


def exchange(value, axis):
    return lax.all_to_all(value, axis, 0, 0, tiled=True)


def gather_small(value, axis, count):
    copies = jnp.broadcast_to(value[None], (count, *value.shape))
    return exchange(copies.reshape(-1, value.shape[1]), axis)


def body(normed_tokens, up_weight, adapter_down, adapter_up, act_grad):
    width = normed_tokens.shape[1]
    hidden = up_weight.shape[1]
    model_index = lax.axis_index("mp")
    core = lax.axis_index("fsdp") & 1
    y_hi, x_at = model_index >> 2, model_index & 3
    one, two = 3 - 2 * core, 1 + 2 * core

    step = [0 * core, one, two, 0 * core + 2]
    table = jnp.stack([((y_hi ^ step[r]) << 2) | (x_at ^ step[q]) for q in range(4) for r in range(4)])

    gathered = lax.all_gather(up_weight, "fsdp", axis=0, tiled=True)

    pair = jnp.concatenate([normed_tokens, y_first(normed_tokens)], axis=1)
    column = jnp.concatenate([pair, y_second(pair)], axis=1)
    near = jnp.concatenate([column, x_first(column)], axis=1)
    far = x_second(near)

    up_columns = lax.dynamic_slice_in_dim(adapter_up, model_index * hidden, hidden, 1)
    low_t, low_term = lowrank_terms(table, near, far, adapter_down.T, up_columns)
    slope_grad, rank_part, up_local, away = forward(
        table, near, far, gathered, low_t, low_term, up_columns, act_grad
    )

    over_x = x_second(away)
    kept = kept_half(table, slope_grad, gathered)
    rank_parts = gather_small(rank_part, "mp", YH * X)
    over_x, kept, rank_parts = lax.optimization_barrier((over_x, kept, rank_parts))

    half = 4 * width
    to_next = (widen(kept[:, half:]) + widen(over_x[:, half:])).astype(bf16)
    over_next = x_first(to_next)
    rank = rank_part.shape[0]
    rank_grad = jnp.sum(widen(rank_parts).reshape(YH * X, rank, -1), axis=0).astype(bf16)
    down_local = jnp.dot(rank_grad, normed_tokens, preferred_element_type=f32).astype(bf16)
    shares = jnp.concatenate(
        [up_local[:, :width], up_local[:, width:], down_local, jnp.zeros_like(down_local)], axis=0
    )
    shares = exchange(shares, "fsdp")
    over_next, shares = lax.optimization_barrier((over_next, shares))

    own = widen(kept[:, :half]) + widen(over_x[:, :half]) + widen(over_next)
    own, to_y = own[:, : 2 * width], own[:, 2 * width :].astype(bf16)
    over_y = y_second(to_y)
    members = Z * YL * C
    share = jnp.sum(widen(shares).reshape(members, -1, width), axis=0).astype(bf16)
    grads = gather_small(share, "fsdp", members)
    over_y, grads = lax.optimization_barrier((over_y, grads))

    own = own + widen(over_y)
    own, to_y = own[:, :width], own[:, width:].astype(bf16)
    summed = own + widen(y_first(to_y))
    up_grad = jnp.concatenate([grads[:rank], grads[rank : 2 * rank]], axis=1)
    down_grad = grads[2 * rank : 3 * rank].T

    down_rows = lax.dynamic_slice_in_dim(adapter_down, model_index * width, width, 0)
    normed_grad = (summed + contract(rank_grad, down_rows, 0, 1)).astype(bf16)
    return (normed_grad, down_grad, up_grad)


def solution(mesh):
    placed = (P("fsdp", "mp"), P("fsdp", "mp"), P(), P(), P("fsdp", "mp"))
    return jax.shard_map(
        body,
        mesh=mesh,
        in_specs=placed,
        out_specs=(P("fsdp", "mp"), P("mp", None), P(None, "mp")),
        check_vma=False,
    )
```

```python
import functools

import jax
import jax.numpy as jnp
from jax import lax
from jax.experimental import pallas as pl
from jax.experimental.pallas import tpu as pltpu
from jax.sharding import PartitionSpec as P

adapter_scale = 2.0
f32, bf16 = jnp.float32, jnp.bfloat16

Z, YL, C = 8, 2, 2
YH, X = 4, 4


def gelu_slope(preact):
    normal_cdf = 0.5 * (1.0 + lax.erf(preact * 0.7071067811865476))
    density = jnp.exp(-0.5 * preact * preact) * 0.3989422804014327
    return normal_cdf + preact * density


def contract(left, right, left_dim, right_dim):
    return lax.dot_general(
        left, right, (((left_dim,), (right_dim,)), ((), ())), preferred_element_type=f32
    )


def send(value, step):
    pairs = []
    for device in range(Z * YL * C * YH * X):
        f, m = device // (YH * X), device % (YH * X)
        z, yl, c, yh, x = step(f // (YL * C), f // C % YL, f % C, m // X, m % X)
        pairs.append((device, ((z * YL + yl) * C + c) * YH * X + yh * X + x))
    return lax.ppermute(value, ("fsdp", "mp"), pairs)


PLANES = [[(z * YL + y) * C + c for z in range(Z) for c in range(C)] for y in range(YL)]


def first(c):
    return 1 if c else 3


def second(c):
    return 3 if c else 1


y_first = functools.partial(send, step=lambda z, yl, c, yh, x: (z, yl, c, yh ^ first(c), x))
y_second = functools.partial(send, step=lambda z, yl, c, yh, x: (z, yl, c, yh ^ second(c), x))
other_plane = functools.partial(send, step=lambda z, yl, c, yh, x: (z, yl ^ 1, c, yh, x))
x_first = functools.partial(send, step=lambda z, yl, c, yh, x: (z, yl, c, yh, x ^ first(c)))
x_second = functools.partial(send, step=lambda z, yl, c, yh, x: (z, yl, c, yh, x ^ second(c)))


def row_copies(lies, w, held, sems, p):
    rows = w.shape[0] // 32
    copies = []
    for run in (2 * p, 2 * p + 1):
        source = w.at[pl.ds(pl.multiple_of(lies[run] * rows, rows), rows)]
        copies.append(pltpu.make_async_copy(source, held.at[pl.ds(run * rows, rows)], sems.at[run]))
    return copies


def start_blocks(lies, w, held, sems, count):
    for p in range(count):
        for copy in row_copies(lies, w, held, sems, p):
            copy.start()


def await_blocks(lies, w, held, sems, first_block):
    for p in (first_block, first_block + 1):
        for copy in row_copies(lies, w, held, sems, p):
            copy.wait()


def lowrank_kernel(table, xa, xb, down_t, up, low_out, term_out):
    width = xa.shape[1] // 8
    low = jnp.zeros(low_out.shape, f32)
    for p in range(16):
        there = pl.ds(pl.multiple_of(table[p] * width, width), width)
        x_ref = xa if p < 8 else xb
        x = x_ref[:, p % 8 * width : (p % 8 + 1) * width]
        low += contract(down_t[:, there], x, 1, 1)
    low_out[...] = low.astype(bf16)
    lowrank = low.T.astype(bf16)
    term_out[...] = adapter_scale * jnp.dot(lowrank, up[...], preferred_element_type=f32)


def main_kernel(lies, xa, xb, w, low_t, term, up, act, slope_out, rank_out, up_out, away, held, acc, sems):
    width = w.shape[0] // 16
    wide = 2 * width
    start_blocks(lies, w, held, sems, 16)

    acc[...] = term[...]
    for k in range(8):
        await_blocks(lies, w, held, sems, 2 * k)
        x_ref = xa if k < 4 else xb
        x = x_ref[:, k % 4 * wide : (k % 4 + 1) * wide]
        acc[...] += jnp.dot(x, held[k * wide : (k + 1) * wide], preferred_element_type=f32)

    slope = (act[...].astype(f32) * gelu_slope(acc[...])).astype(bf16)
    slope_out[...] = slope
    rank_out[...] = (adapter_scale * contract(up[...], slope, 1, 1)).astype(bf16)
    up_out[...] = (adapter_scale * jnp.dot(low_t[...], slope, preferred_element_type=f32)).astype(bf16)

    for k in range(4):
        rows = held[(4 + k) * wide : (5 + k) * wide]
        away[:, k * wide : (k + 1) * wide] = contract(slope, rows, 1, 1).astype(bf16)


VMEM = pl.BlockSpec(memory_space=pltpu.VMEM)
SMEM = pl.BlockSpec(memory_space=pltpu.SMEM)
HBM = pl.BlockSpec(memory_space=pltpu.HBM)


def lowrank_terms(table, xa, xb, down_t, up):
    rows, rank, hidden = xa.shape[0], up.shape[0], up.shape[1]
    return pl.pallas_call(
        lowrank_kernel,
        out_shape=(
            jax.ShapeDtypeStruct((rank, rows), bf16),
            jax.ShapeDtypeStruct((rows, hidden), f32),
        ),
        in_specs=[SMEM, VMEM, VMEM, VMEM, VMEM],
        out_specs=(VMEM, VMEM),
        compiler_params=pltpu.CompilerParams(vmem_limit_bytes=56 * 2**20),
        cost_estimate=pl.CostEstimate(
            flops=2 * rows * rank * 16 * xa.shape[1], bytes_accessed=5 * 2**20, transcendentals=0
        ),
        name="lowrank_terms",
    )(table, xa, xb, down_t, up)


def forward(lies, xa, xb, w, low_t, term, up, act):
    rows, rank, hidden = xa.shape[0], up.shape[0], w.shape[1]
    return pl.pallas_call(
        main_kernel,
        out_shape=(
            jax.ShapeDtypeStruct((rows, hidden), bf16),
            jax.ShapeDtypeStruct((rank, rows), bf16),
            jax.ShapeDtypeStruct((rank, hidden), bf16),
            jax.ShapeDtypeStruct(xa.shape, bf16),
        ),
        in_specs=[SMEM, VMEM, VMEM, HBM, VMEM, VMEM, VMEM, VMEM],
        out_specs=(VMEM, VMEM, VMEM, VMEM),
        scratch_shapes=[
            pltpu.VMEM(w.shape, bf16),
            pltpu.VMEM((rows, hidden), f32),
            pltpu.SemaphoreType.DMA((32,)),
        ],
        compiler_params=pltpu.CompilerParams(vmem_limit_bytes=56 * 2**20),
        cost_estimate=pl.CostEstimate(
            flops=3 * rows * w.shape[0] * hidden, bytes_accessed=14 * 2**20, transcendentals=0
        ),
        name="forward",
    )(lies, xa, xb, w, low_t, term, up, act)


def kept_kernel(lies, slope, w, out, held, sems):
    width = w.shape[0] // 16
    wide = 2 * width
    start_blocks(lies, w, held, sems, 8)
    for k in range(4):
        await_blocks(lies, w, held, sems, 2 * k)
        rows = held[k * wide : (k + 1) * wide]
        out[:, k * wide : (k + 1) * wide] = contract(slope[...], rows, 1, 1).astype(bf16)


def kept_half(lies, slope, w):
    rows, hidden = slope.shape
    half = w.shape[0] // 2
    return pl.pallas_call(
        kept_kernel,
        out_shape=jax.ShapeDtypeStruct((rows, half), bf16),
        in_specs=[SMEM, VMEM, HBM],
        out_specs=VMEM,
        scratch_shapes=[pltpu.VMEM((half, hidden), bf16), pltpu.SemaphoreType.DMA((16,))],
        compiler_params=pltpu.CompilerParams(vmem_limit_bytes=56 * 2**20),
        cost_estimate=pl.CostEstimate(
            flops=2 * rows * half * hidden, bytes_accessed=7 * 2**20, transcendentals=0
        ),
        name="kept_half",
    )(lies, slope, w)


def widen(value):
    return value.astype(f32)


def exchange(value, axis):
    return lax.all_to_all(value, axis, 0, 0, tiled=True)


def gather_small(value, axis, count):
    copies = jnp.broadcast_to(value[None], (count, *value.shape))
    return exchange(copies.reshape(-1, value.shape[1]), axis)


def add_parts(parts, count):
    return jnp.sum(widen(parts).reshape(count, -1, parts.shape[1]), axis=0).astype(bf16)


def body(normed_tokens, up_weight, adapter_down, adapter_up, act_grad):
    width = normed_tokens.shape[1]
    hidden = up_weight.shape[1]
    model_index = lax.axis_index("mp")
    core = lax.axis_index("fsdp") & 1
    y_hi, x_at = model_index >> 2, model_index & 3
    one, two = 3 - 2 * core, 1 + 2 * core

    step = [0 * core, one, two, 0 * core + 2]
    table = jnp.stack([((y_hi ^ step[r]) << 2) | (x_at ^ step[q]) for q in range(4) for r in range(4)])

    plane = (lax.axis_index("fsdp") >> 1) & 1
    both = jnp.concatenate([up_weight, other_plane(up_weight)], axis=0)
    gathered = lax.all_gather(both, "fsdp", axis=0, tiled=True, axis_index_groups=PLANES)
    lies = jnp.stack([(table >> 1) * 4 + ((table & 1) ^ plane) + 2 * c for c in range(C)], axis=1).reshape(-1)

    pair = jnp.concatenate([normed_tokens, y_first(normed_tokens)], axis=1)
    column = jnp.concatenate([pair, y_second(pair)], axis=1)
    near = jnp.concatenate([column, x_first(column)], axis=1)
    far = x_second(near)

    up_columns = lax.dynamic_slice_in_dim(adapter_up, model_index * hidden, hidden, 1)
    low_t, low_term = lowrank_terms(table, near, far, adapter_down.T, up_columns)
    slope_grad, rank_part, up_local, away = forward(
        lies, near, far, gathered, low_t, low_term, up_columns, act_grad
    )

    over_x = x_second(away)
    rank_parts = gather_small(rank_part, "mp", YH * X)
    kept = kept_half(lies, slope_grad, gathered)
    half = 4 * width
    to_next = (widen(kept[:, half:]) + widen(over_x[:, half:])).astype(bf16)
    over_next = x_first(to_next)
    rank_parts, _ = lax.optimization_barrier((rank_parts, to_next))
    rank_grad = add_parts(rank_parts, YH * X)
    rank = rank_grad.shape[0]
    down_local = jnp.dot(rank_grad, normed_tokens, preferred_element_type=f32).astype(bf16)
    shares = jnp.concatenate(
        [up_local[:, :width], up_local[:, width:], down_local, jnp.zeros_like(down_local)], axis=0
    )
    shares = exchange(shares, "fsdp")

    own = widen(kept[:, :half]) + widen(over_x[:, :half]) + widen(over_next)
    own, to_y = own[:, : 2 * width], own[:, 2 * width :].astype(bf16)
    over_y = y_second(to_y)
    shares, _ = lax.optimization_barrier((shares, to_y))
    members = Z * YL * C
    share, over_y = lax.optimization_barrier((add_parts(shares, members), over_y))
    grads = gather_small(share, "fsdp", members)

    own = own + widen(over_y)
    own, to_y = own[:, :width], own[:, width:].astype(bf16)
    over_last = y_first(to_y)
    down_rows = lax.dynamic_slice_in_dim(adapter_down, model_index * width, width, 0)
    own = own + contract(rank_grad, down_rows, 0, 1)
    own, over_last = lax.optimization_barrier((own, over_last))
    normed_grad = (own + widen(over_last)).astype(bf16)
    up_grad = jnp.concatenate([grads[:rank], grads[rank : 2 * rank]], axis=1)
    down_grad = grads[2 * rank : 3 * rank].T
    return (normed_grad, down_grad, up_grad)


def solution(mesh):
    placed = (P("fsdp", "mp"), P("fsdp", "mp"), P(), P(), P("fsdp", "mp"))
    return jax.shard_map(
        body,
        mesh=mesh,
        in_specs=placed,
        out_specs=(P("fsdp", "mp"), P("mp", None), P(None, "mp")),
        check_vma=False,
    )
```

```python
import functools

import jax
import jax.numpy as jnp
from jax import lax
from jax.experimental import pallas as pl
from jax.experimental.pallas import tpu as pltpu
from jax.sharding import PartitionSpec as P

adapter_scale = 2.0
f32, bf16 = jnp.float32, jnp.bfloat16

Z, YL, C = 8, 2, 2
YH, X = 4, 4


def gelu_slope(preact):
    normal_cdf = 0.5 * (1.0 + lax.erf(preact * 0.7071067811865476))
    density = jnp.exp(-0.5 * preact * preact) * 0.3989422804014327
    return normal_cdf + preact * density


def contract(left, right, left_dim, right_dim):
    return lax.dot_general(
        left, right, (((left_dim,), (right_dim,)), ((), ())), preferred_element_type=f32
    )


def send(value, step):
    pairs = []
    for device in range(Z * YL * C * YH * X):
        f, m = device // (YH * X), device % (YH * X)
        z, yl, c, yh, x = step(f // (YL * C), f // C % YL, f % C, m // X, m % X)
        pairs.append((device, ((z * YL + yl) * C + c) * YH * X + yh * X + x))
    return lax.ppermute(value, ("fsdp", "mp"), pairs)


PAIRS = [[z * YL * C + y * C + c for y in range(YL)] for z in range(Z) for c in range(C)]
PLANES = [[(z * YL + y) * C + c for z in range(Z) for c in range(C)] for y in range(YL)]


def first(c):
    return 1 if c else 3


def second(c):
    return 3 if c else 1


y_first = functools.partial(send, step=lambda z, yl, c, yh, x: (z, yl, c, yh ^ first(c), x))
y_second = functools.partial(send, step=lambda z, yl, c, yh, x: (z, yl, c, yh ^ second(c), x))
x_first = functools.partial(send, step=lambda z, yl, c, yh, x: (z, yl, c, yh, x ^ first(c)))
x_second = functools.partial(send, step=lambda z, yl, c, yh, x: (z, yl, c, yh, x ^ second(c)))


def row_copies(lies, w, held, sems, p):
    rows = w.shape[0] // 32
    copies = []
    for run in (2 * p, 2 * p + 1):
        source = w.at[pl.ds(pl.multiple_of(lies[run] * rows, rows), rows)]
        copies.append(pltpu.make_async_copy(source, held.at[pl.ds(run * rows, rows)], sems.at[run]))
    return copies


def start_blocks(lies, w, held, sems, count):
    for p in range(count):
        for copy in row_copies(lies, w, held, sems, p):
            copy.start()


def await_blocks(lies, w, held, sems, first_block):
    for p in (first_block, first_block + 1):
        for copy in row_copies(lies, w, held, sems, p):
            copy.wait()


def lowrank_sum(table, x_ref, down_t, base, low):
    width = x_ref.shape[1] // 8
    for p in range(8):
        there = pl.ds(pl.multiple_of(table[base + p] * width, width), width)
        low += contract(down_t[:, there], x_ref[:, p * width : (p + 1) * width], 1, 1)
    return low


def near_kernel(table, xa, down_t, low_out):
    low_out[...] = lowrank_sum(table, xa, down_t, 0, jnp.zeros(low_out.shape, f32))


def main_kernel(lies, table, xa, xb, w, low_near, down_t, up, act, slope_out, rank_out, up_out, held, acc, sems):
    rank = up.shape[0]
    wide = w.shape[0] // 8
    start_blocks(lies, w, held, sems, 16)

    low_t = lowrank_sum(table, xb, down_t, 8, low_near[...])
    lowrank_t, lowrank = low_t.astype(bf16), low_t.T.astype(bf16)
    acc[...] = adapter_scale * jnp.dot(lowrank, up[...], preferred_element_type=f32)
    for k in range(8):
        await_blocks(lies, w, held, sems, 2 * k)
        x_ref = xa if k < 4 else xb
        x = x_ref[:, k % 4 * wide : (k % 4 + 1) * wide]
        acc[...] += jnp.dot(x, held[k * wide : (k + 1) * wide], preferred_element_type=f32)

    slope = (act[...].astype(f32) * gelu_slope(acc[...])).astype(bf16)
    slope_out[...] = slope
    part = (adapter_scale * contract(up[...], slope, 1, 1)).astype(bf16)
    for copy in range(YH * X):
        rank_out[copy * rank : (copy + 1) * rank] = part
    up_out[...] = (adapter_scale * jnp.dot(lowrank_t, slope, preferred_element_type=f32)).astype(bf16)


VMEM = pl.BlockSpec(memory_space=pltpu.VMEM)
SMEM = pl.BlockSpec(memory_space=pltpu.SMEM)
HBM = pl.BlockSpec(memory_space=pltpu.HBM)


def near_lowrank(table, xa, down_t):
    rows, rank = xa.shape[0], down_t.shape[0]
    return pl.pallas_call(
        near_kernel,
        out_shape=jax.ShapeDtypeStruct((rank, rows), f32),
        in_specs=[SMEM, VMEM, VMEM],
        out_specs=VMEM,
        compiler_params=pltpu.CompilerParams(vmem_limit_bytes=56 * 2**20),
        cost_estimate=pl.CostEstimate(
            flops=2 * rows * rank * xa.shape[1], bytes_accessed=3 * 2**20, transcendentals=0
        ),
        name="near_lowrank",
    )(table, xa, down_t)


def forward(lies, table, xa, xb, w, low_near, down_t, up, act):
    rows, rank, hidden = xa.shape[0], up.shape[0], w.shape[1]
    return pl.pallas_call(
        main_kernel,
        out_shape=(
            jax.ShapeDtypeStruct((rows, hidden), bf16),
            jax.ShapeDtypeStruct((YH * X * rank, rows), bf16),
            jax.ShapeDtypeStruct((rank, hidden), bf16),
        ),
        in_specs=[SMEM, SMEM, VMEM, VMEM, HBM, VMEM, VMEM, VMEM, VMEM],
        out_specs=(VMEM, VMEM, VMEM),
        scratch_shapes=[
            pltpu.VMEM(w.shape, bf16),
            pltpu.VMEM((rows, hidden), f32),
            pltpu.SemaphoreType.DMA((32,)),
        ],
        compiler_params=pltpu.CompilerParams(vmem_limit_bytes=56 * 2**20),
        cost_estimate=pl.CostEstimate(
            flops=2 * rows * w.shape[0] * hidden, bytes_accessed=14 * 2**20, transcendentals=0
        ),
        name="forward",
    )(lies, table, xa, xb, w, low_near, down_t, up, act)


def frozen_kernel(lies, slope, w, kept, away, held, sems):
    wide = w.shape[0] // 8
    start_blocks(lies, w, held, sems, 16)
    for k in range(8):
        await_blocks(lies, w, held, sems, 2 * k)
        out = kept if k < 4 else away
        product = contract(slope[...], held[k * wide : (k + 1) * wide], 1, 1)
        out[:, k % 4 * wide : (k % 4 + 1) * wide] = product.astype(bf16)


def frozen_terms(lies, slope, w):
    rows, hidden = slope.shape
    half = jax.ShapeDtypeStruct((rows, w.shape[0] // 2), bf16)
    return pl.pallas_call(
        frozen_kernel,
        out_shape=(half, half),
        in_specs=[SMEM, VMEM, HBM],
        out_specs=(VMEM, VMEM),
        scratch_shapes=[pltpu.VMEM(w.shape, bf16), pltpu.SemaphoreType.DMA((32,))],
        compiler_params=pltpu.CompilerParams(vmem_limit_bytes=56 * 2**20),
        cost_estimate=pl.CostEstimate(
            flops=2 * rows * w.shape[0] * hidden, bytes_accessed=13 * 2**20, transcendentals=0
        ),
        name="frozen_terms",
    )(lies, slope, w)


def widen(value):
    return value.astype(f32)


def exchange(value, axis):
    return lax.all_to_all(value, axis, 0, 0, tiled=True)


def gather_small(value, axis, count):
    copies = jnp.broadcast_to(value[None], (count, *value.shape))
    return exchange(copies.reshape(-1, value.shape[1]), axis)


def add_parts(parts, count):
    return jnp.sum(widen(parts).reshape(count, -1, parts.shape[1]), axis=0).astype(bf16)


def body(normed_tokens, up_weight, adapter_down, adapter_up, act_grad):
    width = normed_tokens.shape[1]
    hidden = up_weight.shape[1]
    model_index = lax.axis_index("mp")
    core = lax.axis_index("fsdp") & 1
    y_hi, x_at = model_index >> 2, model_index & 3
    one, two = 3 - 2 * core, 1 + 2 * core

    step = [0 * core, one, two, 0 * core + 2]
    table = jnp.stack([((y_hi ^ step[r]) << 2) | (x_at ^ step[q]) for q in range(4) for r in range(4)])

    both = lax.all_gather(up_weight, "fsdp", axis=0, tiled=True, axis_index_groups=PAIRS)
    gathered = lax.all_gather(both, "fsdp", axis=0, tiled=True, axis_index_groups=PLANES)
    lies = jnp.stack([(table >> 1) * 4 + (table & 1) + 2 * c for c in range(C)], axis=1).reshape(-1)

    pair = jnp.concatenate([normed_tokens, y_first(normed_tokens)], axis=1)
    column = jnp.concatenate([pair, y_second(pair)], axis=1)
    near = jnp.concatenate([column, x_first(column)], axis=1)
    far = x_second(near)
    down_t = adapter_down.T
    low_near = near_lowrank(table, near, down_t)

    up_columns = lax.dynamic_slice_in_dim(adapter_up, model_index * hidden, hidden, 1)
    slope_grad, rank_shares, up_local = forward(
        lies, table, near, far, gathered, low_near, down_t, up_columns, act_grad
    )

    rank_parts = exchange(rank_shares, "mp")
    kept, away = frozen_terms(lies, slope_grad, gathered)
    over_x = x_second(away)
    rank_parts, _ = lax.optimization_barrier((rank_parts, away))
    rank_grad = add_parts(rank_parts, YH * X)
    rank = rank_grad.shape[0]
    down_local = jnp.dot(rank_grad, normed_tokens, preferred_element_type=f32).astype(bf16)
    shares = jnp.concatenate(
        [up_local[:, :width], up_local[:, width:], down_local, jnp.zeros_like(down_local)], axis=0
    )
    shares = exchange(shares, "fsdp")

    half = 4 * width
    to_next = (widen(kept[:, half:]) + widen(over_x[:, half:])).astype(bf16)
    over_next = x_first(to_next)
    shares, _ = lax.optimization_barrier((shares, to_next))
    members = Z * YL * C
    grads = gather_small(add_parts(shares, members), "fsdp", members)

    own = widen(kept[:, :half]) + widen(over_x[:, :half]) + widen(over_next)
    own, to_y = own[:, : 2 * width], own[:, 2 * width :].astype(bf16)
    over_y = y_second(to_y)

    own = own + widen(over_y)
    own, to_y = own[:, :width], own[:, width:].astype(bf16)
    over_last = y_first(to_y)
    down_rows = lax.dynamic_slice_in_dim(adapter_down, model_index * width, width, 0)
    own = own + contract(rank_grad, down_rows, 0, 1)
    own, over_last = lax.optimization_barrier((own, over_last))
    normed_grad = (own + widen(over_last)).astype(bf16)
    up_grad = jnp.concatenate([grads[:rank], grads[rank : 2 * rank]], axis=1)
    down_grad = grads[2 * rank : 3 * rank].T
    return (normed_grad, down_grad, up_grad)


def solution(mesh):
    placed = (P("fsdp", "mp"), P("fsdp", "mp"), P(), P(), P("fsdp", "mp"))
    return jax.shard_map(
        body,
        mesh=mesh,
        in_specs=placed,
        out_specs=(P("fsdp", "mp"), P("mp", None), P(None, "mp")),
        check_vma=False,
    )
```

```python
import functools

import jax
import jax.numpy as jnp
from jax import lax
from jax.experimental import pallas as pl
from jax.experimental.pallas import tpu as pltpu
from jax.sharding import PartitionSpec as P

adapter_scale = 2.0
f32, bf16 = jnp.float32, jnp.bfloat16

Z, YL, C = 8, 2, 2
YH, X = 4, 4


def gelu_slope(preact):
    normal_cdf = 0.5 * (1.0 + lax.erf(preact * 0.7071067811865476))
    density = jnp.exp(-0.5 * preact * preact) * 0.3989422804014327
    return normal_cdf + preact * density


def contract(left, right, left_dim, right_dim):
    return lax.dot_general(
        left, right, (((left_dim,), (right_dim,)), ((), ())), preferred_element_type=f32
    )


def send(value, step):
    pairs = []
    for device in range(Z * YL * C * YH * X):
        f, m = device // (YH * X), device % (YH * X)
        z, yl, c, yh, x = step(f // (YL * C), f // C % YL, f % C, m // X, m % X)
        pairs.append((device, ((z * YL + yl) * C + c) * YH * X + yh * X + x))
    return lax.ppermute(value, ("fsdp", "mp"), pairs)


PAIRS = [[z * YL * C + y * C + c for y in range(YL)] for z in range(Z) for c in range(C)]
PLANES = [[(z * YL + y) * C + c for z in range(Z) for c in range(C)] for y in range(YL)]


def first(c):
    return 1 if c else 3


def second(c):
    return 3 if c else 1


y_first = functools.partial(send, step=lambda z, yl, c, yh, x: (z, yl, c, yh ^ first(c), x))
y_second = functools.partial(send, step=lambda z, yl, c, yh, x: (z, yl, c, yh ^ second(c), x))
x_first = functools.partial(send, step=lambda z, yl, c, yh, x: (z, yl, c, yh, x ^ first(c)))
x_second = functools.partial(send, step=lambda z, yl, c, yh, x: (z, yl, c, yh, x ^ second(c)))


def row_copies(lies, w, held, sems, p):
    rows = w.shape[0] // 32
    copies = []
    for run in (2 * p, 2 * p + 1):
        source = w.at[pl.ds(pl.multiple_of(lies[run] * rows, rows), rows)]
        copies.append(pltpu.make_async_copy(source, held.at[pl.ds(run * rows, rows)], sems.at[run]))
    return copies


def start_blocks(lies, w, held, sems, count):
    for p in range(count):
        for copy in row_copies(lies, w, held, sems, p):
            copy.start()


def await_blocks(lies, w, held, sems, first_block):
    for p in (first_block, first_block + 1):
        for copy in row_copies(lies, w, held, sems, p):
            copy.wait()


def lowrank_sum(table, x_ref, down_t, base, low):
    width = x_ref.shape[1] // 8
    for p in range(8):
        there = pl.ds(pl.multiple_of(table[base + p] * width, width), width)
        low += contract(down_t[:, there], x_ref[:, p * width : (p + 1) * width], 1, 1)
    return low


def near_kernel(table, xa, down_t, low_out):
    low_out[...] = lowrank_sum(table, xa, down_t, 0, jnp.zeros(low_out.shape, f32))


def main_kernel(lies, table, xa, xb, w, low_near, down_t, up, act, slope_out, rank_out, up_out, away, held, acc, sems):
    rank = up.shape[0]
    wide = w.shape[0] // 8
    start_blocks(lies, w, held, sems, 16)

    low_t = lowrank_sum(table, xb, down_t, 8, low_near[...])
    lowrank_t, lowrank = low_t.astype(bf16), low_t.T.astype(bf16)
    acc[...] = adapter_scale * jnp.dot(lowrank, up[...], preferred_element_type=f32)
    for k in range(8):
        await_blocks(lies, w, held, sems, 2 * k)
        x_ref = xa if k < 4 else xb
        x = x_ref[:, k % 4 * wide : (k % 4 + 1) * wide]
        acc[...] += jnp.dot(x, held[k * wide : (k + 1) * wide], preferred_element_type=f32)

    slope = (act[...].astype(f32) * gelu_slope(acc[...])).astype(bf16)
    slope_out[...] = slope
    part = (adapter_scale * contract(up[...], slope, 1, 1)).astype(bf16)
    for copy in range(YH * X):
        rank_out[copy * rank : (copy + 1) * rank] = part
    up_out[...] = (adapter_scale * jnp.dot(lowrank_t, slope, preferred_element_type=f32)).astype(bf16)

    for k in range(4):
        rows = held[(4 + k) * wide : (5 + k) * wide]
        away[:, k * wide : (k + 1) * wide] = contract(slope, rows, 1, 1).astype(bf16)


VMEM = pl.BlockSpec(memory_space=pltpu.VMEM)
SMEM = pl.BlockSpec(memory_space=pltpu.SMEM)
HBM = pl.BlockSpec(memory_space=pltpu.HBM)


def near_lowrank(table, xa, down_t):
    rows, rank = xa.shape[0], down_t.shape[0]
    return pl.pallas_call(
        near_kernel,
        out_shape=jax.ShapeDtypeStruct((rank, rows), f32),
        in_specs=[SMEM, VMEM, VMEM],
        out_specs=VMEM,
        compiler_params=pltpu.CompilerParams(vmem_limit_bytes=56 * 2**20),
        cost_estimate=pl.CostEstimate(
            flops=2 * rows * rank * xa.shape[1], bytes_accessed=3 * 2**20, transcendentals=0
        ),
        name="near_lowrank",
    )(table, xa, down_t)


def forward(lies, table, xa, xb, w, low_near, down_t, up, act):
    rows, rank, hidden = xa.shape[0], up.shape[0], w.shape[1]
    return pl.pallas_call(
        main_kernel,
        out_shape=(
            jax.ShapeDtypeStruct((rows, hidden), bf16),
            jax.ShapeDtypeStruct((YH * X * rank, rows), bf16),
            jax.ShapeDtypeStruct((rank, hidden), bf16),
            jax.ShapeDtypeStruct(xa.shape, bf16),
        ),
        in_specs=[SMEM, SMEM, VMEM, VMEM, HBM, VMEM, VMEM, VMEM, VMEM],
        out_specs=(VMEM, VMEM, VMEM, VMEM),
        scratch_shapes=[
            pltpu.VMEM(w.shape, bf16),
            pltpu.VMEM((rows, hidden), f32),
            pltpu.SemaphoreType.DMA((32,)),
        ],
        compiler_params=pltpu.CompilerParams(vmem_limit_bytes=56 * 2**20),
        cost_estimate=pl.CostEstimate(
            flops=3 * rows * w.shape[0] * hidden, bytes_accessed=14 * 2**20, transcendentals=0
        ),
        name="forward",
    )(lies, table, xa, xb, w, low_near, down_t, up, act)


def kept_kernel(lies, slope, w, out, held, sems):
    wide = w.shape[0] // 8
    start_blocks(lies, w, held, sems, 8)
    for k in range(4):
        await_blocks(lies, w, held, sems, 2 * k)
        rows = held[k * wide : (k + 1) * wide]
        out[:, k * wide : (k + 1) * wide] = contract(slope[...], rows, 1, 1).astype(bf16)


def kept_half(lies, slope, w):
    rows, hidden = slope.shape
    half = w.shape[0] // 2
    return pl.pallas_call(
        kept_kernel,
        out_shape=jax.ShapeDtypeStruct((rows, half), bf16),
        in_specs=[SMEM, VMEM, HBM],
        out_specs=VMEM,
        scratch_shapes=[pltpu.VMEM((half, hidden), bf16), pltpu.SemaphoreType.DMA((16,))],
        compiler_params=pltpu.CompilerParams(vmem_limit_bytes=56 * 2**20),
        cost_estimate=pl.CostEstimate(
            flops=2 * rows * half * hidden, bytes_accessed=7 * 2**20, transcendentals=0
        ),
        name="kept_half",
    )(lies, slope, w)


def widen(value):
    return value.astype(f32)


def exchange(value, axis):
    return lax.all_to_all(value, axis, 0, 0, tiled=True)


def gather_small(value, axis, count):
    copies = jnp.broadcast_to(value[None], (count, *value.shape))
    return exchange(copies.reshape(-1, value.shape[1]), axis)


def add_parts(parts, count):
    return jnp.sum(widen(parts).reshape(count, -1, parts.shape[1]), axis=0).astype(bf16)


def body(normed_tokens, up_weight, adapter_down, adapter_up, act_grad):
    width = normed_tokens.shape[1]
    hidden = up_weight.shape[1]
    model_index = lax.axis_index("mp")
    core = lax.axis_index("fsdp") & 1
    y_hi, x_at = model_index >> 2, model_index & 3
    one, two = 3 - 2 * core, 1 + 2 * core

    step = [0 * core, one, two, 0 * core + 2]
    table = jnp.stack([((y_hi ^ step[r]) << 2) | (x_at ^ step[q]) for q in range(4) for r in range(4)])

    both = lax.all_gather(up_weight, "fsdp", axis=0, tiled=True, axis_index_groups=PAIRS)
    gathered = lax.all_gather(both, "fsdp", axis=0, tiled=True, axis_index_groups=PLANES)
    lies = jnp.stack([(table >> 1) * 4 + (table & 1) + 2 * c for c in range(C)], axis=1).reshape(-1)

    pair = jnp.concatenate([normed_tokens, y_first(normed_tokens)], axis=1)
    column = jnp.concatenate([pair, y_second(pair)], axis=1)
    near = jnp.concatenate([column, x_first(column)], axis=1)
    far = x_second(near)
    down_t = adapter_down.T
    low_near = near_lowrank(table, near, down_t)

    up_columns = lax.dynamic_slice_in_dim(adapter_up, model_index * hidden, hidden, 1)
    slope_grad, rank_shares, up_local, away = forward(
        lies, table, near, far, gathered, low_near, down_t, up_columns, act_grad
    )

    over_x = x_second(away)
    rank_parts = exchange(rank_shares, "mp")
    kept = kept_half(lies, slope_grad, gathered)
    half = 4 * width
    to_next = (widen(kept[:, half:]) + widen(over_x[:, half:])).astype(bf16)
    over_next = x_first(to_next)

    rank_parts, _ = lax.optimization_barrier((rank_parts, to_next))
    rank_grad = add_parts(rank_parts, YH * X)
    rank = rank_grad.shape[0]
    down_local = jnp.dot(rank_grad, normed_tokens, preferred_element_type=f32).astype(bf16)
    shares = jnp.concatenate(
        [up_local[:, :width], up_local[:, width:], down_local, jnp.zeros_like(down_local)], axis=0
    )
    shares = exchange(shares, "fsdp")

    own = widen(kept[:, :half]) + widen(over_x[:, :half]) + widen(over_next)
    own, to_y = own[:, : 2 * width], own[:, 2 * width :].astype(bf16)
    over_y = y_second(to_y)
    shares, _ = lax.optimization_barrier((shares, to_y))
    members = Z * YL * C
    grads = gather_small(add_parts(shares, members), "fsdp", members)

    own = own + widen(over_y)
    own, to_y = own[:, :width], own[:, width:].astype(bf16)
    over_last = y_first(to_y)
    down_rows = lax.dynamic_slice_in_dim(adapter_down, model_index * width, width, 0)
    own = own + contract(rank_grad, down_rows, 0, 1)
    own, over_last, grads = lax.optimization_barrier((own, over_last, grads))
    normed_grad = (own + widen(over_last)).astype(bf16)
    up_grad = jnp.concatenate([grads[:rank], grads[rank : 2 * rank]], axis=1)
    down_grad = grads[2 * rank : 3 * rank].T
    return (normed_grad, down_grad, up_grad)


def solution(mesh):
    placed = (P("fsdp", "mp"), P("fsdp", "mp"), P(), P(), P("fsdp", "mp"))
    return jax.shard_map(
        body,
        mesh=mesh,
        in_specs=placed,
        out_specs=(P("fsdp", "mp"), P("mp", None), P(None, "mp")),
        check_vma=False,
    )
```

```python
import functools

import jax
import jax.numpy as jnp
from jax import lax
from jax.experimental import pallas as pl
from jax.experimental.pallas import tpu as pltpu
from jax.sharding import PartitionSpec as P

adapter_scale = 2.0
f32, bf16 = jnp.float32, jnp.bfloat16

Z, YL, C = 8, 2, 2
YH, X = 4, 4


def gelu_slope(preact):
    normal_cdf = 0.5 * (1.0 + lax.erf(preact * 0.7071067811865476))
    density = jnp.exp(-0.5 * preact * preact) * 0.3989422804014327
    return normal_cdf + preact * density


def contract(left, right, left_dim, right_dim):
    return lax.dot_general(
        left, right, (((left_dim,), (right_dim,)), ((), ())), preferred_element_type=f32
    )


def send(value, step):
    pairs = []
    for device in range(Z * YL * C * YH * X):
        f, m = device // (YH * X), device % (YH * X)
        z, yl, c, yh, x = step(f // (YL * C), f // C % YL, f % C, m // X, m % X)
        pairs.append((device, ((z * YL + yl) * C + c) * YH * X + yh * X + x))
    return lax.ppermute(value, ("fsdp", "mp"), pairs)


PAIRS = [[z * YL * C + y * C + c for y in range(YL)] for z in range(Z) for c in range(C)]
PLANES = [[(z * YL + y) * C + c for z in range(Z) for c in range(C)] for y in range(YL)]


def first(c):
    return 1 if c else 3


def second(c):
    return 3 if c else 1


y_first = functools.partial(send, step=lambda z, yl, c, yh, x: (z, yl, c, yh ^ first(c), x))
y_second = functools.partial(send, step=lambda z, yl, c, yh, x: (z, yl, c, yh ^ second(c), x))
x_first = functools.partial(send, step=lambda z, yl, c, yh, x: (z, yl, c, yh, x ^ first(c)))
x_second = functools.partial(send, step=lambda z, yl, c, yh, x: (z, yl, c, yh, x ^ second(c)))


def row_copies(lies, w, held, sems, p):
    rows = w.shape[0] // 32
    copies = []
    for run in (2 * p, 2 * p + 1):
        source = w.at[pl.ds(pl.multiple_of(lies[run] * rows, rows), rows)]
        copies.append(pltpu.make_async_copy(source, held.at[pl.ds(run * rows, rows)], sems.at[run]))
    return copies


def start_blocks(lies, w, held, sems, count):
    for p in range(count):
        for copy in row_copies(lies, w, held, sems, p):
            copy.start()


def await_blocks(lies, w, held, sems, first_block):
    for p in (first_block, first_block + 1):
        for copy in row_copies(lies, w, held, sems, p):
            copy.wait()


def lowrank_sum(table, x_ref, down_t, base, low):
    width = x_ref.shape[1] // 8
    for p in range(8):
        there = pl.ds(pl.multiple_of(table[base + p] * width, width), width)
        low += contract(down_t[:, there], x_ref[:, p * width : (p + 1) * width], 1, 1)
    return low


def near_kernel(table, xa, down_t, low_out):
    low_out[...] = lowrank_sum(table, xa, down_t, 0, jnp.zeros(low_out.shape, f32))


def far_kernel(table, xb, down_t, low_near, up, low_out, term_out):
    low_t = lowrank_sum(table, xb, down_t, 8, low_near[...])
    low_out[...] = low_t.astype(bf16)
    lowrank = low_t.T.astype(bf16)
    term_out[...] = adapter_scale * jnp.dot(lowrank, up[...], preferred_element_type=f32)


def main_kernel(lies, xa, xb, w, low_t, term, up, act, slope_out, rank_out, up_out, away, held, acc, sems):
    rank = up.shape[0]
    wide = w.shape[0] // 8
    start_blocks(lies, w, held, sems, 16)

    acc[...] = term[...]
    for k in range(8):
        await_blocks(lies, w, held, sems, 2 * k)
        x_ref = xa if k < 4 else xb
        x = x_ref[:, k % 4 * wide : (k % 4 + 1) * wide]
        acc[...] += jnp.dot(x, held[k * wide : (k + 1) * wide], preferred_element_type=f32)

    slope = (act[...].astype(f32) * gelu_slope(acc[...])).astype(bf16)
    slope_out[...] = slope
    part = (adapter_scale * contract(up[...], slope, 1, 1)).astype(bf16)
    for copy in range(YH * X):
        rank_out[copy * rank : (copy + 1) * rank] = part
    up_out[...] = (adapter_scale * jnp.dot(low_t[...], slope, preferred_element_type=f32)).astype(bf16)

    for k in range(4):
        rows = held[(4 + k) * wide : (5 + k) * wide]
        away[:, k * wide : (k + 1) * wide] = contract(slope, rows, 1, 1).astype(bf16)


VMEM = pl.BlockSpec(memory_space=pltpu.VMEM)
SMEM = pl.BlockSpec(memory_space=pltpu.SMEM)
HBM = pl.BlockSpec(memory_space=pltpu.HBM)


def near_lowrank(table, xa, down_t):
    rows, rank = xa.shape[0], down_t.shape[0]
    return pl.pallas_call(
        near_kernel,
        out_shape=jax.ShapeDtypeStruct((rank, rows), f32),
        in_specs=[SMEM, VMEM, VMEM],
        out_specs=VMEM,
        compiler_params=pltpu.CompilerParams(vmem_limit_bytes=8 * 2**20),
        cost_estimate=pl.CostEstimate(
            flops=2 * rows * rank * xa.shape[1], bytes_accessed=3 * 2**20, transcendentals=0
        ),
        name="near_lowrank",
    )(table, xa, down_t)


def far_lowrank(table, xb, down_t, low_near, up):
    rows, rank, hidden = xb.shape[0], up.shape[0], up.shape[1]
    return pl.pallas_call(
        far_kernel,
        out_shape=(jax.ShapeDtypeStruct((rank, rows), bf16), jax.ShapeDtypeStruct((rows, hidden), f32)),
        in_specs=[SMEM, VMEM, VMEM, VMEM, VMEM],
        out_specs=(VMEM, VMEM),
        compiler_params=pltpu.CompilerParams(vmem_limit_bytes=8 * 2**20),
        cost_estimate=pl.CostEstimate(
            flops=2 * rows * rank * (xb.shape[1] + hidden), bytes_accessed=4 * 2**20, transcendentals=0
        ),
        name="far_lowrank",
    )(table, xb, down_t, low_near, up)


def forward(lies, xa, xb, w, low_t, term, up, act):
    rows, rank, hidden = xa.shape[0], up.shape[0], w.shape[1]
    return pl.pallas_call(
        main_kernel,
        out_shape=(
            jax.ShapeDtypeStruct((rows, hidden), bf16),
            jax.ShapeDtypeStruct((YH * X * rank, rows), bf16),
            jax.ShapeDtypeStruct((rank, hidden), bf16),
            jax.ShapeDtypeStruct(xa.shape, bf16),
        ),
        in_specs=[SMEM, VMEM, VMEM, HBM, VMEM, VMEM, VMEM, VMEM],
        out_specs=(VMEM, VMEM, VMEM, VMEM),
        scratch_shapes=[
            pltpu.VMEM(w.shape, bf16),
            pltpu.VMEM((rows, hidden), f32),
            pltpu.SemaphoreType.DMA((32,)),
        ],
        compiler_params=pltpu.CompilerParams(vmem_limit_bytes=56 * 2**20),
        cost_estimate=pl.CostEstimate(
            flops=3 * rows * w.shape[0] * hidden, bytes_accessed=14 * 2**20, transcendentals=0
        ),
        name="forward",
    )(lies, xa, xb, w, low_t, term, up, act)


def kept_kernel(lies, slope, w, out, held, sems):
    wide = w.shape[0] // 8
    start_blocks(lies, w, held, sems, 8)
    for k in range(4):
        await_blocks(lies, w, held, sems, 2 * k)
        rows = held[k * wide : (k + 1) * wide]
        out[:, k * wide : (k + 1) * wide] = contract(slope[...], rows, 1, 1).astype(bf16)


def kept_half(lies, slope, w):
    rows, hidden = slope.shape
    half = w.shape[0] // 2
    return pl.pallas_call(
        kept_kernel,
        out_shape=jax.ShapeDtypeStruct((rows, half), bf16),
        in_specs=[SMEM, VMEM, HBM],
        out_specs=VMEM,
        scratch_shapes=[pltpu.VMEM((half, hidden), bf16), pltpu.SemaphoreType.DMA((16,))],
        compiler_params=pltpu.CompilerParams(vmem_limit_bytes=16 * 2**20),
        cost_estimate=pl.CostEstimate(
            flops=2 * rows * half * hidden, bytes_accessed=7 * 2**20, transcendentals=0
        ),
        name="kept_half",
    )(lies, slope, w)


def widen(value):
    return value.astype(f32)


def exchange(value, axis):
    return lax.all_to_all(value, axis, 0, 0, tiled=True)


def gather_small(value, axis, count):
    copies = jnp.broadcast_to(value[None], (count, *value.shape))
    return exchange(copies.reshape(-1, value.shape[1]), axis)


def add_parts(parts, count):
    return jnp.sum(widen(parts).reshape(count, -1, parts.shape[1]), axis=0).astype(bf16)


def body(normed_tokens, up_weight, adapter_down, adapter_up, act_grad):
    width = normed_tokens.shape[1]
    hidden = up_weight.shape[1]
    model_index = lax.axis_index("mp")
    core = lax.axis_index("fsdp") & 1
    y_hi, x_at = model_index >> 2, model_index & 3
    one, two = 3 - 2 * core, 1 + 2 * core

    step = [0 * core, one, two, 0 * core + 2]
    table = jnp.stack([((y_hi ^ step[r]) << 2) | (x_at ^ step[q]) for q in range(4) for r in range(4)])

    both = lax.all_gather(up_weight, "fsdp", axis=0, tiled=True, axis_index_groups=PAIRS)
    gathered = lax.all_gather(both, "fsdp", axis=0, tiled=True, axis_index_groups=PLANES)
    lies = jnp.stack([(table >> 1) * 4 + (table & 1) + 2 * c for c in range(C)], axis=1).reshape(-1)

    pair = jnp.concatenate([normed_tokens, y_first(normed_tokens)], axis=1)
    column = jnp.concatenate([pair, y_second(pair)], axis=1)
    near = jnp.concatenate([column, x_first(column)], axis=1)
    far = x_second(near)
    down_t = adapter_down.T
    low_near = near_lowrank(table, near, down_t)

    up_columns = lax.dynamic_slice_in_dim(adapter_up, model_index * hidden, hidden, 1)
    low_t, low_term = far_lowrank(table, far, down_t, low_near, up_columns)
    slope_grad, rank_shares, up_local, away = forward(
        lies, near, far, gathered, low_t, low_term, up_columns, act_grad
    )

    over_x = x_second(away)
    rank_parts = exchange(rank_shares, "mp")
    kept = kept_half(lies, slope_grad, gathered)
    half = 4 * width
    to_next = (widen(kept[:, half:]) + widen(over_x[:, half:])).astype(bf16)
    over_next = x_first(to_next)

    rank_parts, _ = lax.optimization_barrier((rank_parts, to_next))
    rank_grad = add_parts(rank_parts, YH * X)
    rank = rank_grad.shape[0]
    down_local = jnp.dot(rank_grad, normed_tokens, preferred_element_type=f32).astype(bf16)
    shares = jnp.concatenate(
        [up_local[:, :width], up_local[:, width:], down_local, jnp.zeros_like(down_local)], axis=0
    )
    shares = exchange(shares, "fsdp")

    own = widen(kept[:, :half]) + widen(over_x[:, :half]) + widen(over_next)
    own, to_y = own[:, : 2 * width], own[:, 2 * width :].astype(bf16)
    over_y = y_second(to_y)
    shares, _ = lax.optimization_barrier((shares, to_y))
    members = Z * YL * C
    grads = gather_small(add_parts(shares, members), "fsdp", members)

    own = own + widen(over_y)
    own, to_y = own[:, :width], own[:, width:].astype(bf16)
    over_last = y_first(to_y)
    down_rows = lax.dynamic_slice_in_dim(adapter_down, model_index * width, width, 0)
    own = own + contract(rank_grad, down_rows, 0, 1)
    own, grads = lax.optimization_barrier((own, grads))
    own, over_last = lax.optimization_barrier((own, over_last))
    normed_grad = (own + widen(over_last)).astype(bf16)
    up_grad = jnp.concatenate([grads[:rank], grads[rank : 2 * rank]], axis=1)
    down_grad = grads[2 * rank : 3 * rank].T
    return (normed_grad, down_grad, up_grad)


def solution(mesh):
    placed = (P("fsdp", "mp"), P("fsdp", "mp"), P(), P(), P("fsdp", "mp"))
    return jax.shard_map(
        body,
        mesh=mesh,
        in_specs=placed,
        out_specs=(P("fsdp", "mp"), P("mp", None), P(None, "mp")),
        check_vma=False,
    )
```

```python
import functools

import jax
import jax.numpy as jnp
from jax import lax
from jax.experimental import pallas as pl
from jax.experimental.pallas import tpu as pltpu
from jax.sharding import PartitionSpec as P

adapter_scale = 2.0
f32, bf16 = jnp.float32, jnp.bfloat16

Z, YL, C = 8, 2, 2
YH, X = 4, 4


def gelu_slope(preact):
    normal_cdf = 0.5 * (1.0 + lax.erf(preact * 0.7071067811865476))
    density = jnp.exp(-0.5 * preact * preact) * 0.3989422804014327
    return normal_cdf + preact * density


def contract(left, right, left_dim, right_dim):
    return lax.dot_general(
        left, right, (((left_dim,), (right_dim,)), ((), ())), preferred_element_type=f32
    )


def send(value, step):
    pairs = []
    for device in range(Z * YL * C * YH * X):
        f, m = device // (YH * X), device % (YH * X)
        z, yl, c, yh, x = step(f // (YL * C), f // C % YL, f % C, m // X, m % X)
        pairs.append((device, ((z * YL + yl) * C + c) * YH * X + yh * X + x))
    return lax.ppermute(value, ("fsdp", "mp"), pairs)


PAIRS = [[z * YL * C + y * C + c for y in range(YL)] for z in range(Z) for c in range(C)]
PLANES = [[(z * YL + y) * C + c for z in range(Z) for c in range(C)] for y in range(YL)]


def first(c):
    return 1 if c else 3


def second(c):
    return 3 if c else 1


y_first = functools.partial(send, step=lambda z, yl, c, yh, x: (z, yl, c, yh ^ first(c), x))
y_second = functools.partial(send, step=lambda z, yl, c, yh, x: (z, yl, c, yh ^ second(c), x))
x_first = functools.partial(send, step=lambda z, yl, c, yh, x: (z, yl, c, yh, x ^ first(c)))
x_second = functools.partial(send, step=lambda z, yl, c, yh, x: (z, yl, c, yh, x ^ second(c)))


def row_copies(lies, w, held, sems, p):
    rows = w.shape[0] // 32
    copies = []
    for run in (2 * p, 2 * p + 1):
        source = w.at[pl.ds(pl.multiple_of(lies[run] * rows, rows), rows)]
        copies.append(pltpu.make_async_copy(source, held.at[pl.ds(run * rows, rows)], sems.at[run]))
    return copies


def start_blocks(lies, w, held, sems, count):
    for p in range(count):
        for copy in row_copies(lies, w, held, sems, p):
            copy.start()


def await_blocks(lies, w, held, sems, first_block):
    for p in (first_block, first_block + 1):
        for copy in row_copies(lies, w, held, sems, p):
            copy.wait()


def lowrank_sum(table, x_ref, down_t, base, low):
    width = x_ref.shape[1] // 8
    for p in range(8):
        there = pl.ds(pl.multiple_of(table[base + p] * width, width), width)
        low += contract(down_t[:, there], x_ref[:, p * width : (p + 1) * width], 1, 1)
    return low


def near_kernel(table, xa, down_t, low_out):
    low_out[...] = lowrank_sum(table, xa, down_t, 0, jnp.zeros(low_out.shape, f32))


def far_kernel(table, xb, down_t, low_near, up, low_out, term_out):
    low_t = lowrank_sum(table, xb, down_t, 8, low_near[...])
    low_out[...] = low_t.astype(bf16)
    lowrank = low_t.T.astype(bf16)
    term_out[...] = adapter_scale * jnp.dot(lowrank, up[...], preferred_element_type=f32)


def main_kernel(lies, xa, xb, w, low_t, term, up, act, slope_out, rank_out, up_out, away, held, acc, sems):
    rank = up.shape[0]
    wide = w.shape[0] // 8
    start_blocks(lies, w, held, sems, 16)

    acc[...] = term[...]
    for k in range(8):
        await_blocks(lies, w, held, sems, 2 * k)
        x_ref = xa if k < 4 else xb
        x = x_ref[:, k % 4 * wide : (k % 4 + 1) * wide]
        acc[...] += jnp.dot(x, held[k * wide : (k + 1) * wide], preferred_element_type=f32)

    slope = (act[...].astype(f32) * gelu_slope(acc[...])).astype(bf16)
    slope_out[...] = slope
    part = (adapter_scale * contract(up[...], slope, 1, 1)).astype(bf16)
    for copy in range(YH * X):
        rank_out[copy * rank : (copy + 1) * rank] = part
    up_out[...] = (adapter_scale * jnp.dot(low_t[...], slope, preferred_element_type=f32)).astype(bf16)

    for k in range(4):
        rows = held[(4 + k) * wide : (5 + k) * wide]
        away[:, k * wide : (k + 1) * wide] = contract(slope, rows, 1, 1).astype(bf16)


VMEM = pl.BlockSpec(memory_space=pltpu.VMEM)
SMEM = pl.BlockSpec(memory_space=pltpu.SMEM)
HBM = pl.BlockSpec(memory_space=pltpu.HBM)


def near_lowrank(table, xa, down_t):
    rows, rank = xa.shape[0], down_t.shape[0]
    return pl.pallas_call(
        near_kernel,
        out_shape=jax.ShapeDtypeStruct((rank, rows), f32),
        in_specs=[SMEM, VMEM, VMEM],
        out_specs=VMEM,
        compiler_params=pltpu.CompilerParams(vmem_limit_bytes=8 * 2**20),
        cost_estimate=pl.CostEstimate(
            flops=2 * rows * rank * xa.shape[1], bytes_accessed=3 * 2**20, transcendentals=0
        ),
        name="near_lowrank",
    )(table, xa, down_t)


def far_lowrank(table, xb, down_t, low_near, up):
    rows, rank, hidden = xb.shape[0], up.shape[0], up.shape[1]
    return pl.pallas_call(
        far_kernel,
        out_shape=(jax.ShapeDtypeStruct((rank, rows), bf16), jax.ShapeDtypeStruct((rows, hidden), f32)),
        in_specs=[SMEM, VMEM, VMEM, VMEM, VMEM],
        out_specs=(VMEM, VMEM),
        compiler_params=pltpu.CompilerParams(vmem_limit_bytes=8 * 2**20),
        cost_estimate=pl.CostEstimate(
            flops=2 * rows * rank * (xb.shape[1] + hidden), bytes_accessed=4 * 2**20, transcendentals=0
        ),
        name="far_lowrank",
    )(table, xb, down_t, low_near, up)


def forward(lies, xa, xb, w, low_t, term, up, act):
    rows, rank, hidden = xa.shape[0], up.shape[0], w.shape[1]
    return pl.pallas_call(
        main_kernel,
        out_shape=(
            jax.ShapeDtypeStruct((rows, hidden), bf16),
            jax.ShapeDtypeStruct((YH * X * rank, rows), bf16),
            jax.ShapeDtypeStruct((rank, hidden), bf16),
            jax.ShapeDtypeStruct(xa.shape, bf16),
        ),
        in_specs=[SMEM, VMEM, VMEM, HBM, VMEM, VMEM, VMEM, VMEM],
        out_specs=(VMEM, VMEM, VMEM, VMEM),
        scratch_shapes=[
            pltpu.VMEM(w.shape, bf16),
            pltpu.VMEM((rows, hidden), f32),
            pltpu.SemaphoreType.DMA((32,)),
        ],
        compiler_params=pltpu.CompilerParams(vmem_limit_bytes=56 * 2**20),
        cost_estimate=pl.CostEstimate(
            flops=3 * rows * w.shape[0] * hidden, bytes_accessed=14 * 2**20, transcendentals=0
        ),
        name="forward",
    )(lies, xa, xb, w, low_t, term, up, act)


def kept_kernel(lies, slope, w, out, held, sems):
    wide = w.shape[0] // 8
    start_blocks(lies, w, held, sems, 8)
    for k in range(4):
        await_blocks(lies, w, held, sems, 2 * k)
        rows = held[k * wide : (k + 1) * wide]
        out[:, k * wide : (k + 1) * wide] = contract(slope[...], rows, 1, 1).astype(bf16)


def kept_half(lies, slope, w):
    rows, hidden = slope.shape
    half = w.shape[0] // 2
    return pl.pallas_call(
        kept_kernel,
        out_shape=jax.ShapeDtypeStruct((rows, half), bf16),
        in_specs=[SMEM, VMEM, HBM],
        out_specs=VMEM,
        scratch_shapes=[pltpu.VMEM((half, hidden), bf16), pltpu.SemaphoreType.DMA((16,))],
        compiler_params=pltpu.CompilerParams(vmem_limit_bytes=16 * 2**20),
        cost_estimate=pl.CostEstimate(
            flops=2 * rows * half * hidden, bytes_accessed=7 * 2**20, transcendentals=0
        ),
        name="kept_half",
    )(lies, slope, w)


def widen(value):
    return value.astype(f32)


def exchange(value, axis):
    return lax.all_to_all(value, axis, 0, 0, tiled=True)


def gather_small(value, axis, count):
    copies = jnp.broadcast_to(value[None], (count, *value.shape))
    return exchange(copies.reshape(-1, value.shape[1]), axis)


def total(parts, start, stop):
    return sum(widen(part[:, start:stop]) for part in parts)


def add_parts(parts, count):
    return jnp.sum(widen(parts).reshape(count, -1, parts.shape[1]), axis=0).astype(bf16)


def body(normed_tokens, up_weight, adapter_down, adapter_up, act_grad):
    width = normed_tokens.shape[1]
    hidden = up_weight.shape[1]
    model_index = lax.axis_index("mp")
    core = lax.axis_index("fsdp") & 1
    y_hi, x_at = model_index >> 2, model_index & 3
    one, two = 3 - 2 * core, 1 + 2 * core

    step = [0 * core, one, two, 0 * core + 2]
    table = jnp.stack([((y_hi ^ step[r]) << 2) | (x_at ^ step[q]) for q in range(4) for r in range(4)])

    both = lax.all_gather(up_weight, "fsdp", axis=0, tiled=True, axis_index_groups=PAIRS)
    gathered = lax.all_gather(both, "fsdp", axis=0, tiled=True, axis_index_groups=PLANES)
    lies = jnp.stack([(table >> 1) * 4 + (table & 1) + 2 * c for c in range(C)], axis=1).reshape(-1)

    pair = jnp.concatenate([normed_tokens, y_first(normed_tokens)], axis=1)
    column = jnp.concatenate([pair, y_second(pair)], axis=1)
    near = jnp.concatenate([column, x_first(column)], axis=1)
    far = x_second(near)
    down_t = adapter_down.T
    low_near = near_lowrank(table, near, down_t)

    up_columns = lax.dynamic_slice_in_dim(adapter_up, model_index * hidden, hidden, 1)
    low_t, low_term = far_lowrank(table, far, down_t, low_near, up_columns)
    slope_grad, rank_shares, up_local, away = forward(
        lies, near, far, gathered, low_t, low_term, up_columns, act_grad
    )

    over_x = x_second(away)
    rank_parts = exchange(rank_shares, "mp")
    kept = kept_half(lies, slope_grad, gathered)
    to_next = total([kept, over_x], 4 * width, 8 * width).astype(bf16)
    over_next = x_first(to_next)

    rank_parts, _ = lax.optimization_barrier((rank_parts, to_next))
    rank_grad = add_parts(rank_parts, YH * X)
    rank = rank_grad.shape[0]
    down_local = jnp.dot(rank_grad, normed_tokens, preferred_element_type=f32).astype(bf16)
    shares = jnp.concatenate(
        [up_local[:, :width], up_local[:, width:], down_local, jnp.zeros_like(down_local)], axis=0
    )
    shares = exchange(shares, "fsdp")

    to_y = total([kept, over_x, over_next], 2 * width, 4 * width).astype(bf16)
    over_y = y_second(to_y)
    shares, _ = lax.optimization_barrier((shares, to_y))
    members = Z * YL * C
    grads = gather_small(add_parts(shares, members), "fsdp", members)

    to_last = total([kept, over_x, over_next, over_y], width, 2 * width).astype(bf16)
    over_last = y_first(to_last)
    down_rows = lax.dynamic_slice_in_dim(adapter_down, model_index * width, width, 0)
    own = total([kept, over_x, over_next, over_y], 0, width) + contract(rank_grad, down_rows, 0, 1)
    own, over_last, grads = lax.optimization_barrier((own, over_last, grads))
    normed_grad = (own + widen(over_last)).astype(bf16)
    up_grad = jnp.concatenate([grads[:rank], grads[rank : 2 * rank]], axis=1)
    down_grad = grads[2 * rank : 3 * rank].T
    return (normed_grad, down_grad, up_grad)


def solution(mesh):
    placed = (P("fsdp", "mp"), P("fsdp", "mp"), P(), P(), P("fsdp", "mp"))
    return jax.shard_map(
        body,
        mesh=mesh,
        in_specs=placed,
        out_specs=(P("fsdp", "mp"), P("mp", None), P(None, "mp")),
        check_vma=False,
    )
```

```python
import functools

import jax
import jax.numpy as jnp
from jax import lax
from jax.experimental import pallas as pl
from jax.experimental.pallas import tpu as pltpu
from jax.sharding import PartitionSpec as P

adapter_scale = 2.0
f32, bf16 = jnp.float32, jnp.bfloat16

Z, YL, C = 8, 2, 2
YH, X = 4, 4


def gelu_slope(preact):
    normal_cdf = 0.5 * (1.0 + lax.erf(preact * 0.7071067811865476))
    density = jnp.exp(-0.5 * preact * preact) * 0.3989422804014327
    return normal_cdf + preact * density


def contract(left, right, left_dim, right_dim):
    return lax.dot_general(
        left, right, (((left_dim,), (right_dim,)), ((), ())), preferred_element_type=f32
    )


def send(value, step):
    pairs = []
    for device in range(Z * YL * C * YH * X):
        f, m = device // (YH * X), device % (YH * X)
        z, yl, c, yh, x = step(f // (YL * C), f // C % YL, f % C, m // X, m % X)
        pairs.append((device, ((z * YL + yl) * C + c) * YH * X + yh * X + x))
    return lax.ppermute(value, ("fsdp", "mp"), pairs)


PAIRS = [[z * YL * C + y * C + c for y in range(YL)] for z in range(Z) for c in range(C)]
PLANES = [[(z * YL + y) * C + c for z in range(Z) for c in range(C)] for y in range(YL)]


def first(c):
    return 1 if c else 3


def second(c):
    return 3 if c else 1


y_first = functools.partial(send, step=lambda z, yl, c, yh, x: (z, yl, c, yh ^ first(c), x))
y_second = functools.partial(send, step=lambda z, yl, c, yh, x: (z, yl, c, yh ^ second(c), x))
x_first = functools.partial(send, step=lambda z, yl, c, yh, x: (z, yl, c, yh, x ^ first(c)))
x_second = functools.partial(send, step=lambda z, yl, c, yh, x: (z, yl, c, yh, x ^ second(c)))


def row_copies(lies, w, held, sems, p):
    rows = w.shape[0] // 32
    copies = []
    for run in (2 * p, 2 * p + 1):
        source = w.at[pl.ds(pl.multiple_of(lies[run] * rows, rows), rows)]
        copies.append(pltpu.make_async_copy(source, held.at[pl.ds(run * rows, rows)], sems.at[run]))
    return copies


def start_blocks(lies, w, held, sems, count):
    for p in range(count):
        for copy in row_copies(lies, w, held, sems, p):
            copy.start()


def await_blocks(lies, w, held, sems, first_block):
    for p in (first_block, first_block + 1):
        for copy in row_copies(lies, w, held, sems, p):
            copy.wait()


def lowrank_sum(table, x_ref, down_t, base, low):
    width = x_ref.shape[1] // 8
    for p in range(8):
        there = pl.ds(pl.multiple_of(table[base + p] * width, width), width)
        low += contract(down_t[:, there], x_ref[:, p * width : (p + 1) * width], 1, 1)
    return low


def near_kernel(table, xa, down_t, low_out):
    low_out[...] = lowrank_sum(table, xa, down_t, 0, jnp.zeros(low_out.shape, f32))


def far_kernel(table, xb, down_t, low_near, up, low_out, term_out):
    low_t = lowrank_sum(table, xb, down_t, 8, low_near[...])
    low_out[...] = low_t.astype(bf16)
    lowrank = low_t.T.astype(bf16)
    term_out[...] = adapter_scale * jnp.dot(lowrank, up[...], preferred_element_type=f32)


def main_kernel(lies, xa, xb, w, low_t, term, up, act, slope_out, rank_out, up_out, away, held, acc, sems):
    rank = up.shape[0]
    wide = w.shape[0] // 8
    start_blocks(lies, w, held, sems, 16)

    acc[...] = term[...]
    for k in range(8):
        await_blocks(lies, w, held, sems, 2 * k)
        x_ref = xa if k < 4 else xb
        x = x_ref[:, k % 4 * wide : (k % 4 + 1) * wide]
        acc[...] += jnp.dot(x, held[k * wide : (k + 1) * wide], preferred_element_type=f32)

    slope = (act[...].astype(f32) * gelu_slope(acc[...])).astype(bf16)
    slope_out[...] = slope
    part = (adapter_scale * contract(up[...], slope, 1, 1)).astype(bf16)
    for copy in range(YH * X):
        rank_out[copy * rank : (copy + 1) * rank] = part
    up_out[...] = (adapter_scale * jnp.dot(low_t[...], slope, preferred_element_type=f32)).astype(bf16)

    for k in range(4):
        rows = held[(4 + k) * wide : (5 + k) * wide]
        away[:, k * wide : (k + 1) * wide] = contract(slope, rows, 1, 1).astype(bf16)


VMEM = pl.BlockSpec(memory_space=pltpu.VMEM)
SMEM = pl.BlockSpec(memory_space=pltpu.SMEM)
HBM = pl.BlockSpec(memory_space=pltpu.HBM)


def near_lowrank(table, xa, down_t):
    rows, rank = xa.shape[0], down_t.shape[0]
    return pl.pallas_call(
        near_kernel,
        out_shape=jax.ShapeDtypeStruct((rank, rows), f32),
        in_specs=[SMEM, VMEM, VMEM],
        out_specs=VMEM,
        compiler_params=pltpu.CompilerParams(vmem_limit_bytes=8 * 2**20),
        cost_estimate=pl.CostEstimate(
            flops=2 * rows * rank * xa.shape[1], bytes_accessed=3 * 2**20, transcendentals=0
        ),
        name="near_lowrank",
    )(table, xa, down_t)


def far_lowrank(table, xb, down_t, low_near, up):
    rows, rank, hidden = xb.shape[0], up.shape[0], up.shape[1]
    return pl.pallas_call(
        far_kernel,
        out_shape=(jax.ShapeDtypeStruct((rank, rows), bf16), jax.ShapeDtypeStruct((rows, hidden), f32)),
        in_specs=[SMEM, VMEM, VMEM, VMEM, VMEM],
        out_specs=(VMEM, VMEM),
        compiler_params=pltpu.CompilerParams(vmem_limit_bytes=8 * 2**20),
        cost_estimate=pl.CostEstimate(
            flops=2 * rows * rank * (xb.shape[1] + hidden), bytes_accessed=4 * 2**20, transcendentals=0
        ),
        name="far_lowrank",
    )(table, xb, down_t, low_near, up)


def forward(lies, xa, xb, w, low_t, term, up, act):
    rows, rank, hidden = xa.shape[0], up.shape[0], w.shape[1]
    return pl.pallas_call(
        main_kernel,
        out_shape=(
            jax.ShapeDtypeStruct((rows, hidden), bf16),
            jax.ShapeDtypeStruct((YH * X * rank, rows), bf16),
            jax.ShapeDtypeStruct((rank, hidden), bf16),
            jax.ShapeDtypeStruct(xa.shape, bf16),
        ),
        in_specs=[SMEM, VMEM, VMEM, HBM, VMEM, VMEM, VMEM, VMEM],
        out_specs=(VMEM, VMEM, VMEM, VMEM),
        scratch_shapes=[
            pltpu.VMEM(w.shape, bf16),
            pltpu.VMEM((rows, hidden), f32),
            pltpu.SemaphoreType.DMA((32,)),
        ],
        compiler_params=pltpu.CompilerParams(vmem_limit_bytes=56 * 2**20),
        cost_estimate=pl.CostEstimate(
            flops=3 * rows * w.shape[0] * hidden, bytes_accessed=14 * 2**20, transcendentals=0
        ),
        name="forward",
    )(lies, xa, xb, w, low_t, term, up, act)


def kept_kernel(lies, slope, w, out, held, sems):
    wide = w.shape[0] // 8
    start_blocks(lies, w, held, sems, 8)
    for k in range(4):
        await_blocks(lies, w, held, sems, 2 * k)
        rows = held[k * wide : (k + 1) * wide]
        out[:, k * wide : (k + 1) * wide] = contract(slope[...], rows, 1, 1).astype(bf16)


def kept_half(lies, slope, w):
    rows, hidden = slope.shape
    half = w.shape[0] // 2
    return pl.pallas_call(
        kept_kernel,
        out_shape=jax.ShapeDtypeStruct((rows, half), bf16),
        in_specs=[SMEM, VMEM, HBM],
        out_specs=VMEM,
        scratch_shapes=[pltpu.VMEM((half, hidden), bf16), pltpu.SemaphoreType.DMA((16,))],
        compiler_params=pltpu.CompilerParams(vmem_limit_bytes=16 * 2**20),
        cost_estimate=pl.CostEstimate(
            flops=2 * rows * half * hidden, bytes_accessed=7 * 2**20, transcendentals=0
        ),
        name="kept_half",
    )(lies, slope, w)


def widen(value):
    return value.astype(f32)


def exchange(value, axis):
    return lax.all_to_all(value, axis, 0, 0, tiled=True)


def gather_small(value, axis, count):
    copies = jnp.broadcast_to(value[None], (count, *value.shape))
    return exchange(copies.reshape(-1, value.shape[1]), axis)


def total(parts, start, stop):
    return sum(widen(part[:, start:stop]) for part in parts)


def add_parts(parts, count):
    return jnp.sum(widen(parts).reshape(count, -1, parts.shape[1]), axis=0).astype(bf16)


def body(normed_tokens, up_weight, adapter_down, adapter_up, act_grad):
    width = normed_tokens.shape[1]
    hidden = up_weight.shape[1]
    model_index = lax.axis_index("mp")
    core = lax.axis_index("fsdp") & 1
    y_hi, x_at = model_index >> 2, model_index & 3
    one, two = 3 - 2 * core, 1 + 2 * core

    step = [0 * core, one, two, 0 * core + 2]
    table = jnp.stack([((y_hi ^ step[r]) << 2) | (x_at ^ step[q]) for q in range(4) for r in range(4)])

    both = lax.all_gather(up_weight, "fsdp", axis=0, tiled=True, axis_index_groups=PAIRS)
    both, next_y = lax.optimization_barrier((both, y_first(normed_tokens)))
    gathered = lax.all_gather(both, "fsdp", axis=0, tiled=True, axis_index_groups=PLANES)
    lies = jnp.stack([(table >> 1) * 4 + (table & 1) + 2 * c for c in range(C)], axis=1).reshape(-1)

    pair = jnp.concatenate([normed_tokens, next_y], axis=1)
    column = jnp.concatenate([pair, y_second(pair)], axis=1)
    near = jnp.concatenate([column, x_first(column)], axis=1)
    far = x_second(near)
    down_t = adapter_down.T
    low_near = near_lowrank(table, near, down_t)

    up_columns = lax.dynamic_slice_in_dim(adapter_up, model_index * hidden, hidden, 1)
    low_t, low_term = far_lowrank(table, far, down_t, low_near, up_columns)
    slope_grad, rank_shares, up_local, away = forward(
        lies, near, far, gathered, low_t, low_term, up_columns, act_grad
    )

    over_x = x_second(away)
    rank_parts = exchange(rank_shares, "mp")
    kept = kept_half(lies, slope_grad, gathered)
    to_next = total([kept, over_x], 4 * width, 8 * width).astype(bf16)
    over_next = x_first(to_next)

    rank_parts, _ = lax.optimization_barrier((rank_parts, to_next))
    rank_grad = add_parts(rank_parts, YH * X)
    rank = rank_grad.shape[0]
    down_local = jnp.dot(rank_grad, normed_tokens, preferred_element_type=f32).astype(bf16)
    shares = jnp.concatenate(
        [up_local[:, :width], up_local[:, width:], down_local, jnp.zeros_like(down_local)], axis=0
    )
    shares = exchange(shares, "fsdp")

    to_y = total([kept, over_x, over_next], 2 * width, 4 * width).astype(bf16)
    over_y = y_second(to_y)
    shares, _ = lax.optimization_barrier((shares, to_y))
    members = Z * YL * C
    grads = gather_small(add_parts(shares, members), "fsdp", members)

    own = total([kept, over_x, over_next], 0, 2 * width)
    to_last = (own[:, width:] + widen(over_y[:, width:])).astype(bf16)
    over_last = y_first(to_last)
    down_rows = lax.dynamic_slice_in_dim(adapter_down, model_index * width, width, 0)
    own = own[:, :width] + widen(over_y[:, :width]) + contract(rank_grad, down_rows, 0, 1)
    own, over_last, grads = lax.optimization_barrier((own, over_last, grads))
    normed_grad = (own + widen(over_last)).astype(bf16)
    up_grad = jnp.concatenate([grads[:rank], grads[rank : 2 * rank]], axis=1)
    down_grad = grads[2 * rank : 3 * rank].T
    return (normed_grad, down_grad, up_grad)


def solution(mesh):
    placed = (P("fsdp", "mp"), P("fsdp", "mp"), P(), P(), P("fsdp", "mp"))
    return jax.shard_map(
        body,
        mesh=mesh,
        in_specs=placed,
        out_specs=(P("fsdp", "mp"), P("mp", None), P(None, "mp")),
        check_vma=False,
    )
```

```python
import functools

import jax
import jax.numpy as jnp
from jax import lax
from jax.experimental import pallas as pl
from jax.experimental.pallas import tpu as pltpu
from jax.sharding import PartitionSpec as P

adapter_scale = 2.0
f32, bf16 = jnp.float32, jnp.bfloat16

Z, YL, C = 8, 2, 2
YH, X = 4, 4


def gelu_slope(preact):
    normal_cdf = 0.5 * (1.0 + lax.erf(preact * 0.7071067811865476))
    density = jnp.exp(-0.5 * preact * preact) * 0.3989422804014327
    return normal_cdf + preact * density


def contract(left, right, left_dim, right_dim):
    return lax.dot_general(
        left, right, (((left_dim,), (right_dim,)), ((), ())), preferred_element_type=f32
    )


def send(value, step):
    pairs = []
    for device in range(Z * YL * C * YH * X):
        f, m = device // (YH * X), device % (YH * X)
        z, yl, c, yh, x = step(f // (YL * C), f // C % YL, f % C, m // X, m % X)
        pairs.append((device, ((z * YL + yl) * C + c) * YH * X + yh * X + x))
    return lax.ppermute(value, ("fsdp", "mp"), pairs)


PAIRS = [[z * YL * C + y * C + c for y in range(YL)] for z in range(Z) for c in range(C)]
PLANES = [[(z * YL + y) * C + c for z in range(Z) for c in range(C)] for y in range(YL)]


def first(c):
    return 1 if c else 3


def second(c):
    return 3 if c else 1


y_first = functools.partial(send, step=lambda z, yl, c, yh, x: (z, yl, c, yh ^ first(c), x))
y_second = functools.partial(send, step=lambda z, yl, c, yh, x: (z, yl, c, yh ^ second(c), x))
x_first = functools.partial(send, step=lambda z, yl, c, yh, x: (z, yl, c, yh, x ^ first(c)))
x_second = functools.partial(send, step=lambda z, yl, c, yh, x: (z, yl, c, yh, x ^ second(c)))


def row_copies(lies, w, held, sems, p):
    rows = w.shape[0] // 32
    copies = []
    for run in (2 * p, 2 * p + 1):
        source = w.at[pl.ds(pl.multiple_of(lies[run] * rows, rows), rows)]
        copies.append(pltpu.make_async_copy(source, held.at[pl.ds(run * rows, rows)], sems.at[run]))
    return copies


def start_blocks(lies, w, held, sems, count):
    for p in range(count):
        for copy in row_copies(lies, w, held, sems, p):
            copy.start()


def await_blocks(lies, w, held, sems, first_block):
    for p in (first_block, first_block + 1):
        for copy in row_copies(lies, w, held, sems, p):
            copy.wait()


def lowrank_sum(table, x_ref, down_t, base, low):
    width = x_ref.shape[1] // 8
    for p in range(8):
        there = pl.ds(pl.multiple_of(table[base + p] * width, width), width)
        low += contract(down_t[:, there], x_ref[:, p * width : (p + 1) * width], 1, 1)
    return low


def near_kernel(table, xa, down_t, low_out):
    low_out[...] = lowrank_sum(table, xa, down_t, 0, jnp.zeros(low_out.shape, f32))


def far_kernel(table, xb, down_t, low_near, up, low_out, term_out):
    low_t = lowrank_sum(table, xb, down_t, 8, low_near[...])
    low_out[...] = low_t.astype(bf16)
    lowrank = low_t.T.astype(bf16)
    term_out[...] = adapter_scale * jnp.dot(lowrank, up[...], preferred_element_type=f32)


def main_kernel(lies, xa, xb, w, low_t, term, up, act, slope_out, rank_out, up_out, away, held, acc, sems):
    rank = up.shape[0]
    wide = w.shape[0] // 8
    start_blocks(lies, w, held, sems, 16)

    acc[...] = term[...]
    for k in range(8):
        await_blocks(lies, w, held, sems, 2 * k)
        x_ref = xa if k < 4 else xb
        x = x_ref[:, k % 4 * wide : (k % 4 + 1) * wide]
        acc[...] += jnp.dot(x, held[k * wide : (k + 1) * wide], preferred_element_type=f32)

    slope = (act[...].astype(f32) * gelu_slope(acc[...])).astype(bf16)
    slope_out[...] = slope
    part = (adapter_scale * contract(up[...], slope, 1, 1)).astype(bf16)
    for copy in range(YH * X):
        rank_out[copy * rank : (copy + 1) * rank] = part
    up_out[...] = (adapter_scale * jnp.dot(low_t[...], slope, preferred_element_type=f32)).astype(bf16)

    for k in range(4):
        rows = held[(4 + k) * wide : (5 + k) * wide]
        away[:, k * wide : (k + 1) * wide] = contract(slope, rows, 1, 1).astype(bf16)


VMEM = pl.BlockSpec(memory_space=pltpu.VMEM)
SMEM = pl.BlockSpec(memory_space=pltpu.SMEM)
HBM = pl.BlockSpec(memory_space=pltpu.HBM)


def near_lowrank(table, xa, down_t):
    rows, rank = xa.shape[0], down_t.shape[0]
    return pl.pallas_call(
        near_kernel,
        out_shape=jax.ShapeDtypeStruct((rank, rows), f32),
        in_specs=[SMEM, VMEM, VMEM],
        out_specs=VMEM,
        compiler_params=pltpu.CompilerParams(vmem_limit_bytes=8 * 2**20),
        cost_estimate=pl.CostEstimate(
            flops=2 * rows * rank * xa.shape[1], bytes_accessed=3 * 2**20, transcendentals=0
        ),
        name="near_lowrank",
    )(table, xa, down_t)


def far_lowrank(table, xb, down_t, low_near, up):
    rows, rank, hidden = xb.shape[0], up.shape[0], up.shape[1]
    return pl.pallas_call(
        far_kernel,
        out_shape=(jax.ShapeDtypeStruct((rank, rows), bf16), jax.ShapeDtypeStruct((rows, hidden), f32)),
        in_specs=[SMEM, VMEM, VMEM, VMEM, VMEM],
        out_specs=(VMEM, VMEM),
        compiler_params=pltpu.CompilerParams(vmem_limit_bytes=56 * 2**20),
        cost_estimate=pl.CostEstimate(
            flops=2 * rows * rank * (xb.shape[1] + hidden), bytes_accessed=4 * 2**20, transcendentals=0
        ),
        name="far_lowrank",
    )(table, xb, down_t, low_near, up)


def forward(lies, xa, xb, w, low_t, term, up, act):
    rows, rank, hidden = xa.shape[0], up.shape[0], w.shape[1]
    return pl.pallas_call(
        main_kernel,
        out_shape=(
            jax.ShapeDtypeStruct((rows, hidden), bf16),
            jax.ShapeDtypeStruct((YH * X * rank, rows), bf16),
            jax.ShapeDtypeStruct((rank, hidden), bf16),
            jax.ShapeDtypeStruct(xa.shape, bf16),
        ),
        in_specs=[SMEM, VMEM, VMEM, HBM, VMEM, VMEM, VMEM, VMEM],
        out_specs=(VMEM, VMEM, VMEM, VMEM),
        scratch_shapes=[
            pltpu.VMEM(w.shape, bf16),
            pltpu.VMEM((rows, hidden), f32),
            pltpu.SemaphoreType.DMA((32,)),
        ],
        compiler_params=pltpu.CompilerParams(vmem_limit_bytes=56 * 2**20),
        cost_estimate=pl.CostEstimate(
            flops=3 * rows * w.shape[0] * hidden, bytes_accessed=14 * 2**20, transcendentals=0
        ),
        name="forward",
    )(lies, xa, xb, w, low_t, term, up, act)


def kept_kernel(lies, slope, w, out, held, sems):
    wide = w.shape[0] // 8
    start_blocks(lies, w, held, sems, 8)
    for k in range(4):
        await_blocks(lies, w, held, sems, 2 * k)
        rows = held[k * wide : (k + 1) * wide]
        out[:, k * wide : (k + 1) * wide] = contract(slope[...], rows, 1, 1).astype(bf16)


def kept_half(lies, slope, w):
    rows, hidden = slope.shape
    half = w.shape[0] // 2
    return pl.pallas_call(
        kept_kernel,
        out_shape=jax.ShapeDtypeStruct((rows, half), bf16),
        in_specs=[SMEM, VMEM, HBM],
        out_specs=VMEM,
        scratch_shapes=[pltpu.VMEM((half, hidden), bf16), pltpu.SemaphoreType.DMA((16,))],
        compiler_params=pltpu.CompilerParams(vmem_limit_bytes=16 * 2**20),
        cost_estimate=pl.CostEstimate(
            flops=2 * rows * half * hidden, bytes_accessed=7 * 2**20, transcendentals=0
        ),
        name="kept_half",
    )(lies, slope, w)


def widen(value):
    return value.astype(f32)


def exchange(value, axis):
    return lax.all_to_all(value, axis, 0, 0, tiled=True)


def gather_small(value, axis, count):
    copies = jnp.broadcast_to(value[None], (count, *value.shape))
    return exchange(copies.reshape(-1, value.shape[1]), axis)


def total(parts, start, stop):
    return sum(widen(part[:, start:stop]) for part in parts)


def add_parts(parts, count):
    return jnp.sum(widen(parts).reshape(count, -1, parts.shape[1]), axis=0).astype(bf16)


def body(normed_tokens, up_weight, adapter_down, adapter_up, act_grad):
    width = normed_tokens.shape[1]
    hidden = up_weight.shape[1]
    model_index = lax.axis_index("mp")
    core = lax.axis_index("fsdp") & 1
    y_hi, x_at = model_index >> 2, model_index & 3
    one, two = 3 - 2 * core, 1 + 2 * core

    step = [0 * core, one, two, 0 * core + 2]
    table = jnp.stack([((y_hi ^ step[r]) << 2) | (x_at ^ step[q]) for q in range(4) for r in range(4)])

    both = lax.all_gather(up_weight, "fsdp", axis=0, tiled=True, axis_index_groups=PAIRS)
    gathered = lax.all_gather(both, "fsdp", axis=0, tiled=True, axis_index_groups=PLANES)
    lies = jnp.stack([(table >> 1) * 4 + (table & 1) + 2 * c for c in range(C)], axis=1).reshape(-1)

    pair = jnp.concatenate([normed_tokens, y_first(normed_tokens)], axis=1)
    column = jnp.concatenate([pair, y_second(pair)], axis=1)
    near = jnp.concatenate([column, x_first(column)], axis=1)
    far = x_second(near)
    down_t = adapter_down.T
    low_near = near_lowrank(table, near, down_t)

    up_columns = lax.dynamic_slice_in_dim(adapter_up, model_index * hidden, hidden, 1)
    low_t, low_term = far_lowrank(table, far, down_t, low_near, up_columns)
    slope_grad, rank_shares, up_local, away = forward(
        lies, near, far, gathered, low_t, low_term, up_columns, act_grad
    )

    over_x = x_second(away)
    rank_parts = exchange(rank_shares, "mp")
    kept = kept_half(lies, slope_grad, gathered)
    to_next = total([kept, over_x], 4 * width, 8 * width).astype(bf16)
    over_next = x_first(to_next)

    rank_parts, _ = lax.optimization_barrier((rank_parts, to_next))
    rank_grad = add_parts(rank_parts, YH * X)
    rank = rank_grad.shape[0]
    down_local = jnp.dot(rank_grad, normed_tokens, preferred_element_type=f32).astype(bf16)
    shares = jnp.concatenate(
        [up_local[:, :width], up_local[:, width:], down_local, jnp.zeros_like(down_local)], axis=0
    )
    shares = exchange(shares, "fsdp")

    to_y = total([kept, over_x, over_next], 2 * width, 4 * width).astype(bf16)
    over_y = y_second(to_y)
    shares, _ = lax.optimization_barrier((shares, to_y))
    members = Z * YL * C
    grads = gather_small(add_parts(shares, members), "fsdp", members)

    own = total([kept, over_x, over_next], 0, 2 * width)
    to_last = (own[:, width:] + widen(over_y[:, width:])).astype(bf16)
    over_last = y_first(to_last)
    down_rows = lax.dynamic_slice_in_dim(adapter_down, model_index * width, width, 0)
    own = own[:, :width] + widen(over_y[:, :width]) + contract(rank_grad, down_rows, 0, 1)
    own, over_last, grads = lax.optimization_barrier((own, over_last, grads))
    normed_grad = (own + widen(over_last)).astype(bf16)
    up_grad = jnp.concatenate([grads[:rank], grads[rank : 2 * rank]], axis=1)
    down_grad = grads[2 * rank : 3 * rank].T
    return (normed_grad, down_grad, up_grad)


def solution(mesh):
    placed = (P("fsdp", "mp"), P("fsdp", "mp"), P(), P(), P("fsdp", "mp"))
    return jax.shard_map(
        body,
        mesh=mesh,
        in_specs=placed,
        out_specs=(P("fsdp", "mp"), P("mp", None), P(None, "mp")),
        check_vma=False,
    )
```

```python
import functools

import jax
import jax.numpy as jnp
from jax import lax
from jax.experimental import pallas as pl
from jax.experimental.pallas import tpu as pltpu
from jax.sharding import PartitionSpec as P

adapter_scale = 2.0
f32, bf16 = jnp.float32, jnp.bfloat16

Z, YL, C = 8, 2, 2
YH, X = 4, 4


def gelu_slope(preact):
    normal_cdf = 0.5 * (1.0 + lax.erf(preact * 0.7071067811865476))
    density = jnp.exp(-0.5 * preact * preact) * 0.3989422804014327
    return normal_cdf + preact * density


def contract(left, right, left_dim, right_dim):
    return lax.dot_general(
        left, right, (((left_dim,), (right_dim,)), ((), ())), preferred_element_type=f32
    )


def send(value, step):
    pairs = []
    for device in range(Z * YL * C * YH * X):
        f, m = device // (YH * X), device % (YH * X)
        z, yl, c, yh, x = step(f // (YL * C), f // C % YL, f % C, m // X, m % X)
        pairs.append((device, ((z * YL + yl) * C + c) * YH * X + yh * X + x))
    return lax.ppermute(value, ("fsdp", "mp"), pairs)


PAIRS = [[z * YL * C + y * C + c for y in range(YL)] for z in range(Z) for c in range(C)]
PLANES = [[(z * YL + y) * C + c for z in range(Z) for c in range(C)] for y in range(YL)]


def first(c):
    return 1 if c else 3


def second(c):
    return 3 if c else 1


y_first = functools.partial(send, step=lambda z, yl, c, yh, x: (z, yl, c, yh ^ first(c), x))
y_second = functools.partial(send, step=lambda z, yl, c, yh, x: (z, yl, c, yh ^ second(c), x))
x_first = functools.partial(send, step=lambda z, yl, c, yh, x: (z, yl, c, yh, x ^ first(c)))
x_second = functools.partial(send, step=lambda z, yl, c, yh, x: (z, yl, c, yh, x ^ second(c)))


def row_copies(lies, w, held, sems, p):
    rows = w.shape[0] // 32
    copies = []
    for run in (2 * p, 2 * p + 1):
        source = w.at[pl.ds(pl.multiple_of(lies[run] * rows, rows), rows)]
        copies.append(pltpu.make_async_copy(source, held.at[pl.ds(run * rows, rows)], sems.at[run]))
    return copies


def start_blocks(lies, w, held, sems, count):
    for p in range(count):
        for copy in row_copies(lies, w, held, sems, p):
            copy.start()


def await_blocks(lies, w, held, sems, first_block):
    for p in (first_block, first_block + 1):
        for copy in row_copies(lies, w, held, sems, p):
            copy.wait()


def lowrank_sum(table, x_ref, down_t, base, low):
    width = x_ref.shape[1] // 8
    for p in range(8):
        there = pl.ds(pl.multiple_of(table[base + p] * width, width), width)
        low += contract(down_t[:, there], x_ref[:, p * width : (p + 1) * width], 1, 1)
    return low


def near_kernel(table, xa, down_t, low_out):
    low_out[...] = lowrank_sum(table, xa, down_t, 0, jnp.zeros(low_out.shape, f32))


def far_kernel(table, xb, down_t, low_near, up, low_out, term_out):
    low_t = lowrank_sum(table, xb, down_t, 8, low_near[...])
    low_out[...] = low_t.astype(bf16)
    lowrank = low_t.T.astype(bf16)
    term_out[...] = adapter_scale * jnp.dot(lowrank, up[...], preferred_element_type=f32)


def main_kernel(lies, xa, xb, w, low_t, term, up, act, slope_out, rank_out, up_out, away, held, acc, sems):
    rank = up.shape[0]
    wide = w.shape[0] // 8
    start_blocks(lies, w, held, sems, 16)

    acc[...] = term[...]
    for k in range(8):
        await_blocks(lies, w, held, sems, 2 * k)
        x_ref = xa if k < 4 else xb
        x = x_ref[:, k % 4 * wide : (k % 4 + 1) * wide]
        acc[...] += jnp.dot(x, held[k * wide : (k + 1) * wide], preferred_element_type=f32)

    slope = (act[...].astype(f32) * gelu_slope(acc[...])).astype(bf16)
    slope_out[...] = slope
    part = (adapter_scale * contract(up[...], slope, 1, 1)).astype(bf16)
    for copy in range(YH * X):
        rank_out[copy * rank : (copy + 1) * rank] = part
    up_out[...] = (adapter_scale * jnp.dot(low_t[...], slope, preferred_element_type=f32)).astype(bf16)

    for k in range(4):
        rows = held[(4 + k) * wide : (5 + k) * wide]
        away[:, k * wide : (k + 1) * wide] = contract(slope, rows, 1, 1).astype(bf16)


VMEM = pl.BlockSpec(memory_space=pltpu.VMEM)
SMEM = pl.BlockSpec(memory_space=pltpu.SMEM)
HBM = pl.BlockSpec(memory_space=pltpu.HBM)


def near_lowrank(table, xa, down_t):
    rows, rank = xa.shape[0], down_t.shape[0]
    return pl.pallas_call(
        near_kernel,
        out_shape=jax.ShapeDtypeStruct((rank, rows), f32),
        in_specs=[SMEM, VMEM, VMEM],
        out_specs=VMEM,
        compiler_params=pltpu.CompilerParams(vmem_limit_bytes=8 * 2**20),
        cost_estimate=pl.CostEstimate(
            flops=2 * rows * rank * xa.shape[1], bytes_accessed=3 * 2**20, transcendentals=0
        ),
        name="near_lowrank",
    )(table, xa, down_t)


def far_lowrank(table, xb, down_t, low_near, up):
    rows, rank, hidden = xb.shape[0], up.shape[0], up.shape[1]
    return pl.pallas_call(
        far_kernel,
        out_shape=(jax.ShapeDtypeStruct((rank, rows), bf16), jax.ShapeDtypeStruct((rows, hidden), f32)),
        in_specs=[SMEM, VMEM, VMEM, VMEM, VMEM],
        out_specs=(VMEM, VMEM),
        compiler_params=pltpu.CompilerParams(vmem_limit_bytes=56 * 2**20),
        cost_estimate=pl.CostEstimate(
            flops=2 * rows * rank * (xb.shape[1] + hidden), bytes_accessed=4 * 2**20, transcendentals=0
        ),
        name="far_lowrank",
    )(table, xb, down_t, low_near, up)


def forward(lies, xa, xb, w, low_t, term, up, act):
    rows, rank, hidden = xa.shape[0], up.shape[0], w.shape[1]
    return pl.pallas_call(
        main_kernel,
        out_shape=(
            jax.ShapeDtypeStruct((rows, hidden), bf16),
            jax.ShapeDtypeStruct((YH * X * rank, rows), bf16),
            jax.ShapeDtypeStruct((rank, hidden), bf16),
            jax.ShapeDtypeStruct(xa.shape, bf16),
        ),
        in_specs=[SMEM, VMEM, VMEM, HBM, VMEM, VMEM, VMEM, VMEM],
        out_specs=(VMEM, VMEM, VMEM, VMEM),
        scratch_shapes=[
            pltpu.VMEM(w.shape, bf16),
            pltpu.VMEM((rows, hidden), f32),
            pltpu.SemaphoreType.DMA((32,)),
        ],
        compiler_params=pltpu.CompilerParams(vmem_limit_bytes=56 * 2**20),
        cost_estimate=pl.CostEstimate(
            flops=3 * rows * w.shape[0] * hidden, bytes_accessed=14 * 2**20, transcendentals=0
        ),
        name="forward",
    )(lies, xa, xb, w, low_t, term, up, act)


def kept_kernel(lies, slope, w, out, held, sems):
    wide = w.shape[0] // 8
    start_blocks(lies, w, held, sems, 8)
    for k in range(4):
        await_blocks(lies, w, held, sems, 2 * k)
        rows = held[k * wide : (k + 1) * wide]
        out[:, k * wide : (k + 1) * wide] = contract(slope[...], rows, 1, 1).astype(bf16)


def kept_half(lies, slope, w):
    rows, hidden = slope.shape
    half = w.shape[0] // 2
    return pl.pallas_call(
        kept_kernel,
        out_shape=jax.ShapeDtypeStruct((rows, half), bf16),
        in_specs=[SMEM, VMEM, HBM],
        out_specs=VMEM,
        scratch_shapes=[pltpu.VMEM((half, hidden), bf16), pltpu.SemaphoreType.DMA((16,))],
        compiler_params=pltpu.CompilerParams(vmem_limit_bytes=56 * 2**20),
        cost_estimate=pl.CostEstimate(
            flops=2 * rows * half * hidden, bytes_accessed=7 * 2**20, transcendentals=0
        ),
        name="kept_half",
    )(lies, slope, w)


def widen(value):
    return value.astype(f32)


def exchange(value, axis):
    return lax.all_to_all(value, axis, 0, 0, tiled=True)


def gather_small(value, axis, count):
    copies = jnp.broadcast_to(value[None], (count, *value.shape))
    return exchange(copies.reshape(-1, value.shape[1]), axis)


def add_parts(parts, count):
    return jnp.sum(widen(parts).reshape(count, -1, parts.shape[1]), axis=0).astype(bf16)


def body(normed_tokens, up_weight, adapter_down, adapter_up, act_grad):
    width = normed_tokens.shape[1]
    hidden = up_weight.shape[1]
    model_index = lax.axis_index("mp")
    core = lax.axis_index("fsdp") & 1
    y_hi, x_at = model_index >> 2, model_index & 3
    one, two = 3 - 2 * core, 1 + 2 * core

    step = [0 * core, one, two, 0 * core + 2]
    table = jnp.stack([((y_hi ^ step[r]) << 2) | (x_at ^ step[q]) for q in range(4) for r in range(4)])

    both = lax.all_gather(up_weight, "fsdp", axis=0, tiled=True, axis_index_groups=PAIRS)
    gathered = lax.all_gather(both, "fsdp", axis=0, tiled=True, axis_index_groups=PLANES)
    lies = jnp.stack([(table >> 1) * 4 + (table & 1) + 2 * c for c in range(C)], axis=1).reshape(-1)

    pair = jnp.concatenate([normed_tokens, y_first(normed_tokens)], axis=1)
    column = jnp.concatenate([pair, y_second(pair)], axis=1)
    near = jnp.concatenate([column, x_first(column)], axis=1)
    far = x_second(near)
    down_t = adapter_down.T
    low_near = near_lowrank(table, near, down_t)

    up_columns = lax.dynamic_slice_in_dim(adapter_up, model_index * hidden, hidden, 1)
    low_t, low_term = far_lowrank(table, far, down_t, low_near, up_columns)
    slope_grad, rank_shares, up_local, away = forward(
        lies, near, far, gathered, low_t, low_term, up_columns, act_grad
    )

    over_x = x_second(away)
    rank_parts = exchange(rank_shares, "mp")
    kept = kept_half(lies, slope_grad, gathered)
    half = 4 * width
    to_next = (widen(kept[:, half:]) + widen(over_x[:, half:])).astype(bf16)
    over_next = x_first(to_next)

    rank_parts, _ = lax.optimization_barrier((rank_parts, to_next))
    rank_grad = add_parts(rank_parts, YH * X)
    rank = rank_grad.shape[0]
    down_local = jnp.dot(rank_grad, normed_tokens, preferred_element_type=f32).astype(bf16)
    shares = jnp.concatenate(
        [up_local[:, :width], up_local[:, width:], down_local, jnp.zeros_like(down_local)], axis=0
    )
    shares = exchange(shares, "fsdp")

    own = widen(kept[:, :half]) + widen(over_x[:, :half]) + widen(over_next)
    own, to_y = own[:, : 2 * width], own[:, 2 * width :].astype(bf16)
    over_y = y_second(to_y)
    shares, _ = lax.optimization_barrier((shares, to_y))
    members = Z * YL * C
    grads = gather_small(add_parts(shares, members), "fsdp", members)

    own = own + widen(over_y)
    own, to_y = own[:, :width], own[:, width:].astype(bf16)
    over_last = y_first(to_y)
    down_rows = lax.dynamic_slice_in_dim(adapter_down, model_index * width, width, 0)
    own = own + contract(rank_grad, down_rows, 0, 1)
    own, over_last, grads = lax.optimization_barrier((own, over_last, grads))
    normed_grad = (own + widen(over_last)).astype(bf16)
    up_grad = jnp.concatenate([grads[:rank], grads[rank : 2 * rank]], axis=1)
    down_grad = grads[2 * rank : 3 * rank].T
    return (normed_grad, down_grad, up_grad)


def solution(mesh):
    placed = (P("fsdp", "mp"), P("fsdp", "mp"), P(), P(), P("fsdp", "mp"))
    return jax.shard_map(
        body,
        mesh=mesh,
        in_specs=placed,
        out_specs=(P("fsdp", "mp"), P("mp", None), P(None, "mp")),
        check_vma=False,
    )
```
